256 devices in a mesh: feat: 128 (over z, x, y), rep: 2 (over core).
Axes of the slice: x: 4, y: 4, z: 8, core: 2. Of those that a mesh axis runs over, the one named last changes fastest.
Arguments:
- inputs: bfloat16 [1024, 440], P('rep'), may hold values from -6 to 6
- targets: bfloat16 [1024, 512], P('rep'), may hold values from -6 to 6
- frequencies: bfloat16 [440, 524288], P(None, ('feat', 'rep')), may hold values from -1.5 to 1.5
- phases: float32 [524288], P(('feat', 'rep')), may hold values from 0 to 6.2832
- weights: bfloat16 [524288, 512], P(('feat', 'rep')), may hold values from -6 to 6
- eigvecs: bfloat16 [524288, 256], P(('feat', 'rep')), may hold values from -0.125 to 0.125
- eigvals: float32 [256], replicated, may hold values from 0.1 to 1
- tail: float32 [1], replicated, may hold values from 0.02 to 0.08
Outputs:
- new_weights: bfloat16 [524288, 512], P(('feat', 'rep'))
- residual: float32 [1024, 512], P(None, ('feat', 'rep'))
The draws below stay inside these ranges and needn't reach their ends.
All inputs are finite; a program needn't handle non-finite values.
Results may differ from the reference program's by a relative error of at most 0.0045.
Values may be sent and summed in bfloat16 or wider, within the bound.
A program may use at most 64 MiB of HBM per device.

```python
import math
import jax
import jax.numpy as jnp
from jax import lax

D_IN = 440
TARGETS = 512
EIGS = 256
FEAT_DEV = 2048
BATCH = 1024
FEATURES = 524288


def steps_of(stream_key, extent, shards, least, high):
    loudness = 1.0
    for dim, blocks in shards:
        steps = jax.random.uniform(jax.random.fold_in(jax.random.fold_in(stream_key, 6), dim), (blocks,), jnp.float32, least / len(shards), high / len(shards))
        loudness = loudness * jnp.repeat(jnp.exp(steps), extent[dim] // blocks).reshape((-1,) + (1,) * (len(extent) - 1 - dim))
    return loudness


def normal_values(rng, extent, width, most, cuts=(), dtype=jnp.bfloat16):
    level = steps_of(rng, extent, cuts, -0.22, 0.18) if cuts else 1.0
    drawn = jax.random.normal(rng, extent, jnp.float32) * width * level
    return jnp.minimum(jnp.maximum(drawn, -most), most).astype(dtype)


def setup_inputs(seed: int = 0) -> dict:
    arg_keys = jax.random.split(jax.random.key(seed), 9)
    inputs = normal_values(arg_keys[0], (BATCH, D_IN), 1.0, 6.0, ((0, 2),))
    targets = normal_values(arg_keys[1], (BATCH, TARGETS), 1.0, 6.0, ((0, 2),))
    frequencies = normal_values(arg_keys[2], (D_IN, FEATURES), 0.1, 1.5, ((1, 256),))
    phases = jnp.clip(6.2832 * jax.random.uniform(arg_keys[3], (FEATURES,), jnp.float32) ** steps_of(arg_keys[3], (FEATURES,), ((0, 256),), -0.2, 0.2), 0.0, 6.2832)
    weights = normal_values(arg_keys[4], (FEATURES, TARGETS), 1.0, 6.0, ((0, 256),))
    eigvecs = normal_values(arg_keys[5], (FEATURES, EIGS), (1.0 / (EIGS * FEATURES) ** 0.25), 0.125, ((0, 256),))
    eigvals = jnp.clip(jnp.exp(jax.random.uniform(arg_keys[6], (EIGS,), jnp.float32, math.log(0.1), math.log(1.0))), 0.1, 1.0)
    tail = jnp.clip(jnp.exp(jax.random.uniform(arg_keys[7], (1,), jnp.float32, math.log(0.02), math.log(0.08))), 0.02, 0.08)
    return dict(inputs=inputs, targets=targets, frequencies=frequencies, phases=phases, weights=weights, eigvecs=eigvecs, eigvals=eigvals, tail=tail)


def reference(inputs, targets, frequencies, phases, weights, eigvecs, eigvals, tail):
    group = 16
    block = FEAT_DEV * group
    nblocks = FEATURES // block
    scale = math.sqrt(2.0 / FEATURES)
    freq_blocks = frequencies.reshape(D_IN, nblocks, block).transpose(1, 0, 2)
    phase_blocks = phases.reshape(nblocks, block)
    weight_blocks = weights.reshape(nblocks, block, TARGETS)
    eigen_blocks = eigvecs.reshape(nblocks, block, EIGS)

    def featurize(freq_part, phase_part):
        theta = jnp.dot(inputs, freq_part, preferred_element_type=jnp.float32) + phase_part[None, :]
        return (scale * jnp.cos(theta)).astype(jnp.bfloat16)

    def predict_step(carry, pieces):
        freq_part, phase_part, weight_part = pieces
        feats = featurize(freq_part, phase_part)
        return (carry + jnp.dot(feats, weight_part, preferred_element_type=jnp.float32), None)
    pred, unused = lax.scan(predict_step, jnp.zeros((BATCH, TARGETS), jnp.float32), (freq_blocks, phase_blocks, weight_blocks))
    residual = pred - targets.astype(jnp.float32)
    resid_b = residual.astype(jnp.bfloat16)

    def grad_step(carry, pieces):
        freq_part, phase_part, eigen_part = pieces
        feats = featurize(freq_part, phase_part)
        grad = lax.dot_general(feats, resid_b, (((0,), (0,)), ((), ())), preferred_element_type=jnp.float32)
        term = jnp.dot(eigen_part.astype(jnp.float32).T, grad, precision=lax.Precision.HIGHEST)
        return (carry + term, grad)
    coeff, grads = lax.scan(grad_step, jnp.zeros((EIGS, TARGETS), jnp.float32), (freq_blocks, phase_blocks, eigen_blocks))
    grads = grads.reshape(FEATURES, TARGETS)
    damp = 1.0 - tail[0] / eigvals
    correction = jnp.dot(eigvecs.astype(jnp.float32), damp[:, None] * coeff, precision=lax.Precision.HIGHEST)
    new_weights = weights.astype(jnp.float32) - (grads - correction) / tail[0]
    return (new_weights.astype(jnp.bfloat16), residual)
```

```python
import functools
import math

import jax
import jax.numpy as jnp
from jax import lax
from jax.experimental import pallas as pl
from jax.experimental.pallas import tpu as pltpu
from jax.sharding import PartitionSpec as P

MESH = pl.DeviceIdType.MESH
BF, F32 = jnp.bfloat16, jnp.float32
FEATURES = 524288
SCALE = math.sqrt(2.0 / FEATURES)
INV_TURN = 1.0 / (2.0 * math.pi)
SIN = (6.283164044300404, -41.33714237083565, 81.34076887918835, -70.99343319450264)
NP = 4


def scaled_cos(theta, turns):
    t = theta * INV_TURN + turns
    s = 0.25 - jnp.abs(t - jnp.round(t))
    u = s * s
    p = SIN[3] * SCALE
    for q in SIN[2::-1]:
        p = p * u + q * SCALE
    return (s * p).astype(BF)


def kernel(
    in_hbm, targ_hbm, freq_hbm, w_hbm, e_hbm, phase_ref, eig_ref, tail_ref,
    out_hbm, res_hbm,
    x_v, freq_v, we_v, targ_v, scale_v, feat_v, ft_v, g_v,
    own_v, send_c, recv_c, buf_a, recv_a, own_b, buf_b, recv_b, recv_z,
    gath, rk_v, out_v, res_v,
    load_sem, store_sem, sx, rx, sc, rc, sa, ra, sb, rb, sz, rz, sgb, rgb, sga, rga, sgc, rgc,
):
    f, c = lax.axis_index("feat"), lax.axis_index("rep")
    z, x, y = f // 16, (f // 4) % 4, f % 4

    def at_x(d):
        return (z * 16 + ((x + d) % 4) * 4 + y, c)

    def at_y(d):
        return (z * 16 + x * 4 + (y + d) % 4, c)

    def at_z(d):
        return (((z + d) % 8) * 16 + x * 4 + y, c)

    mate = (f, 1 - c)
    barrier = pltpu.get_barrier_semaphore()
    everyone = [mate]
    everyone += [at_x(d) for d in (1, 2, 3)] + [at_y(d) for d in (1, 2, 3)]
    everyone += [at_z(d) for d in range(1, 8)]
    for peer in everyone:
        pl.semaphore_signal(barrier, inc=1, device_id=peer, device_id_type=MESH)

    loads = [
        (in_hbm, x_v.at[0]),
        (freq_hbm, freq_v),
        (w_hbm, we_v.at[:, 0:512]),
        (e_hbm, we_v.at[:, 512:768]),
        (targ_hbm.at[:, 0:384], targ_v.at[0]),
        (targ_hbm.at[:, 384:512], targ_v.at[1, :, 0:128]),
    ]
    loads = [pltpu.make_async_copy(s, d, load_sem.at[i]) for i, (s, d) in enumerate(loads)]
    for load in loads:
        load.start()
    targ_v[1, :, 128:384] = jnp.zeros((512, 256), BF)
    scale_v[...] = jnp.ones_like(scale_v)
    scale_v[1, :, 128:384] = 1.0 - tail_ref[...] / eig_ref[...]

    def remote(src, dst, send, recv, peer):
        return pltpu.make_async_remote_copy(
            src_ref=src, dst_ref=dst, send_sem=send, recv_sem=recv,
            device_id=peer, device_id_type=MESH,
        )

    def first(p):
        return (x, at_x) if p % 2 == 0 else (y, at_y)

    def second(p):
        return (y, at_y) if p % 2 == 0 else (x, at_x)

    def core_copy(p):
        return remote(send_c.at[p], recv_c.at[p], sc.at[p], rc.at[p], mate)

    def a_copies(p):
        i, peer = first(p)
        return [
            remote(buf_a.at[p, pl.ds(((i + d) % 4) * 4, 4)], recv_a.at[p, d - 1], sa.at[p, d - 1], ra.at[p, d - 1], peer(d))
            for d in (1, 2, 3)
        ]

    def b_copies(p):
        i, peer = second(p)
        return [
            remote(buf_b.at[p, (i + d) % 4], recv_b.at[p, d - 1], sb.at[p, d - 1], rb.at[p, d - 1], peer(d))
            for d in (1, 2, 3)
        ]

    def z_copies(p):
        return [
            remote(recv_z.at[p, z], recv_z.at[p, z], sz.at[p, d - 1], rz.at[p, d - 1], at_z(d))
            for d in range(1, 8)
        ]

    def gb_copies(p):
        i, (k, peer) = first(p)[0], second(p)
        here = gath.at[p, 0, i * 4 + k]
        return [remote(here, here, sgb.at[p, d - 1], rgb.at[p, d - 1], peer(d)) for d in (1, 2, 3)]

    def ga_copies(p):
        i, peer = first(p)
        here = gath.at[p, 0, pl.ds(i * 4, 4)]
        return [remote(here, here, sga.at[p, d - 1], rga.at[p, d - 1], peer(d)) for d in (1, 2, 3)]

    def gc_copy(p):
        return remote(gath.at[p, 0], gath.at[p, 1], sgc.at[p], rgc.at[p], mate)

    def start(copies):
        for copy in copies:
            copy.start()

    def arrived(copies):
        for copy in copies:
            copy.wait_recv()

    def sent(copies):
        for copy in copies:
            copy.wait_send()

    turns = phase_ref[...] * INV_TURN

    def features(half, pair):
        def tile(n, carry):
            cols = pl.ds(pl.multiple_of(n * 1024, 1024), 1024)
            theta = jnp.dot(x_v[half, pl.ds(pair * 256, 256), :], freq_v[:, cols], preferred_element_type=F32)
            value = scaled_cos(theta, phase_ref[:, cols] * INV_TURN)
            for q in (0, 1):
                feat_v[2 * pair + q, pl.ds(half * 128, 128), cols] = value[q * 128:(q + 1) * 128]
            return carry

        lax.fori_loop(0, 2, tile, 0)

    def project(p):
        def tile(n, carry):
            cols = pl.ds(pl.multiple_of(n * 256, 256), 256)
            part = jnp.dot(feat_v[p], we_v[:, cols], preferred_element_type=F32)
            own_v[p, :, cols] = part[0:128]
            send_c[p, :, cols] = part[128:256].astype(BF)
            return carry

        lax.fori_loop(0, 3, tile, 0)
        core_copy(p).start()

    def stage_1(p):
        arrived([core_copy(p)])
        for i in range(4):
            for j in range(2):
                rows = pl.ds(32 * i + 16 * j, 16)
                total = own_v[p, rows, :] + recv_c[p, rows, :].astype(F32)
                own_v[p, rows, :] = total
                for k in range(2):
                    buf_a[p, 4 * i + 2 * j + k] = total[:, 384 * k:384 * (k + 1)].astype(BF)
        start(a_copies(p))
        sent([core_copy(p)])

    def stage_2(p):
        arrived(a_copies(p))
        i = first(p)[0]
        for j in range(2):
            rows = pl.ds(pl.multiple_of(32 * i + 16 * j, 16), 16)
            for k in range(2):
                b = 2 * j + k
                total = own_v[p, rows, 384 * k:384 * (k + 1)]
                for d in range(3):
                    total = total + recv_a[p, d, b].astype(F32)
                own_b[p, b] = total
                buf_b[p, b] = total.astype(BF)
        start(b_copies(p))
        sent(a_copies(p))

    def stage_3(p):
        arrived(b_copies(p))
        k = second(p)[0]
        total = own_b[p, k]
        for d in range(3):
            total = total + recv_b[p, d].astype(F32)
        recv_z[p, z] = total.astype(BF)
        start(z_copies(p))
        sent(b_copies(p))

    def stage_4(p):
        arrived(z_copies(p))
        i, k = first(p)[0], second(p)[0]
        total = recv_z[p, 0].astype(F32)
        for d in range(1, 8):
            total = total + recv_z[p, d].astype(F32)
        rows = pl.ds(pl.multiple_of(p * 128 + 32 * i + 16 * (k // 2), 16), 16)
        total = total * scale_v[k % 2] - targ_v[k % 2, rows, :].astype(F32)
        gath[p, 0, i * 4 + k] = total.astype(BF)
        start(gb_copies(p))
        sent(z_copies(p))

    def stage_5(p):
        arrived(gb_copies(p))
        start(ga_copies(p))
        sent(gb_copies(p))

    def stage_6(p):
        arrived(ga_copies(p))
        gc_copy(p).start()
        sent(ga_copies(p))

    column = 4 * f + 2 * c

    def stage_7(p):
        arrived([gc_copy(p)])
        for half in range(2):
            for b in range(16):
                rows = half * 128 + 32 * (b // 4) + 16 * ((b % 4) // 2)
                rk_v[p, rows:rows + 16, 384 * (b % 2):384 * (b % 2 + 1)] = gath[p, half, b]
        sent([gc_copy(p)])
        pick = lax.broadcasted_iota(jnp.int32, (8, 512), 1) == lax.broadcasted_iota(jnp.int32, (8, 512), 0) + column
        pick = jnp.where(pick, 1.0, 0.0).astype(BF)
        shown = lax.dot_general(pick, rk_v[p, :, 0:512], (((1,), (1,)), ((), ())), preferred_element_type=F32)
        for half in range(2):
            res_v[half, :, p * 128:(p + 1) * 128] = shown[:, half * 128:(half + 1) * 128]
        resid = rk_v[p, :, 0:512]
        coeff = lax.dot_general(
            rk_v[p, :, 512:768], resid, (((0,), (0,)), ((), ())), preferred_element_type=F32
        )
        coeff = (-coeff).astype(BF)
        last = p == NP - 1
        rate = 1.0 / tail_ref[...]

        def tile(n, carry):
            rows = pl.ds(pl.multiple_of(n * 512, 512), 512)
            part = jnp.dot(ft_v[p, rows, :], resid, preferred_element_type=F32)
            part = part + jnp.dot(we_v[rows, 512:768], coeff, preferred_element_type=F32)
            if p > 0:
                part = part + g_v[rows, :]
            if last:
                out_v[rows, :] = (we_v[rows, 0:512].astype(F32) - part * rate).astype(BF)
                pltpu.make_async_copy(out_v.at[rows], out_hbm.at[rows], store_sem.at[n]).start()
            else:
                g_v[rows, :] = part
            return carry

        lax.fori_loop(0, 4, tile, 0)

    def flip(p):
        def tile(n, carry):
            cols = pl.ds(pl.multiple_of(n * 256, 256), 256)
            ft_v[p, cols, :] = feat_v[p, :, cols].T
            return carry

        lax.fori_loop(0, 8, tile, 0)

    loads[0].wait()
    loads[1].wait()
    features(0, 0)
    pl.semaphore_wait(barrier, len(everyone))
    trade = remote(in_hbm, x_v.at[1], sx, rx, mate)
    trade.start()
    features(0, 1)
    for load in loads[2:]:
        load.wait()
    trade.wait()
    features(1, 0)
    project(0)
    project(1)
    stage_1(0)
    features(1, 1)
    stage_1(1)
    project(2)
    project(3)
    stage_1(2)
    stage_2(0)
    stage_1(3)
    flip(0)
    stage_2(1)
    flip(1)
    stage_3(0)
    stage_2(2)
    flip(2)
    stage_3(1)
    stage_2(3)
    flip(3)
    stage_4(0)
    stage_3(2)
    stage_4(1)
    stage_3(3)
    stage_5(0)
    stage_4(2)
    stage_5(1)
    stage_4(3)
    stage_6(0)
    stage_5(2)
    stage_6(1)
    stage_5(3)
    stage_7(0)
    stage_6(2)
    stage_7(1)
    stage_6(3)
    stage_7(2)
    stage_7(3)
    shown = [
        pltpu.make_async_copy(res_v.at[0], res_hbm.at[c], store_sem.at[4]),
        pltpu.make_async_copy(res_v.at[1], res_hbm.at[1 - c], store_sem.at[5]),
    ]
    start(shown)
    for n in range(4):
        rows = pl.ds(n * 512, 512)
        pltpu.make_async_copy(out_v.at[rows], out_hbm.at[rows], store_sem.at[n]).wait()
    for copy in shown:
        copy.wait()


def shards(inputs, targets, frequencies, phases, weights, eigvecs, eigvals, tail):
    hbm = pl.BlockSpec(memory_space=pl.ANY)
    vmem = pl.BlockSpec(memory_space=pltpu.VMEM)
    dma = pltpu.SemaphoreType.DMA
    chunk = (16, 384)
    new_weights, shown = pl.pallas_call(
        kernel,
        out_shape=[
            jax.ShapeDtypeStruct((2048, 512), BF),
            jax.ShapeDtypeStruct((2, 8, 512), F32),
        ],
        in_specs=[hbm] * 5 + [vmem] * 3,
        out_specs=[hbm, hbm],
        scratch_shapes=[
            pltpu.VMEM((2, 512, 440), BF),
            pltpu.VMEM((440, 2048), BF),
            pltpu.VMEM((2048, 768), BF),
            pltpu.VMEM((2, 512, 384), BF),
            pltpu.VMEM((2, 1, 384), F32),
            pltpu.VMEM((NP, 256, 2048), BF),
            pltpu.VMEM((NP, 2048, 256), BF),
            pltpu.VMEM((2048, 512), F32),
            pltpu.VMEM((NP, 128, 768), F32),
            pltpu.VMEM((NP, 128, 768), BF),
            pltpu.VMEM((NP, 128, 768), BF),
            pltpu.VMEM((NP, 16) + chunk, BF),
            pltpu.VMEM((NP, 3, 4) + chunk, BF),
            pltpu.VMEM((NP, 4) + chunk, F32),
            pltpu.VMEM((NP, 4) + chunk, BF),
            pltpu.VMEM((NP, 3) + chunk, BF),
            pltpu.VMEM((NP, 8) + chunk, BF),
            pltpu.VMEM((NP, 2, 16) + chunk, BF),
            pltpu.VMEM((NP, 256, 768), BF),
            pltpu.VMEM((2048, 512), BF),
            pltpu.VMEM((2, 8, 512), F32),
            dma((6,)), dma((6,)),
            dma, dma,
            dma((NP,)), dma((NP,)),
            dma((NP, 3)), dma((NP, 3)),
            dma((NP, 3)), dma((NP, 3)),
            dma((NP, 7)), dma((NP, 7)),
            dma((NP, 3)), dma((NP, 3)),
            dma((NP, 3)), dma((NP, 3)),
            dma((NP,)), dma((NP,)),
        ],
        compiler_params=pltpu.CompilerParams(
            collective_id=0, has_side_effects=True, vmem_limit_bytes=60 << 20
        ),
        name="step",
    )(
        inputs, targets, frequencies, weights, eigvecs,
        phases.reshape(1, -1), eigvals.reshape(1, -1), tail.reshape(1, 1),
    )
    residual = shown[:, 0:2, :].transpose(0, 2, 1).reshape(1024, 2)
    return (new_weights, residual)


def solution(mesh):
    in_specs = (
        P("rep", None),
        P("rep", None),
        P(None, ("feat", "rep")),
        P(("feat", "rep")),
        P(("feat", "rep"), None),
        P(("feat", "rep"), None),
        P(),
        P(),
    )
    out_specs = (P(("feat", "rep"), None), P(None, ("feat", "rep")))
    return jax.shard_map(shards, mesh=mesh, in_specs=in_specs, out_specs=out_specs, check_vma=False)
```

```python
import functools
import math

import jax
import jax.numpy as jnp
from jax import lax
from jax.experimental import pallas as pl
from jax.experimental.pallas import tpu as pltpu
from jax.sharding import PartitionSpec as P

MESH = pl.DeviceIdType.MESH
BF, F32 = jnp.bfloat16, jnp.float32
FEATURES = 524288
SCALE = math.sqrt(2.0 / FEATURES)
INV_TURN = 1.0 / (2.0 * math.pi)
SIN = (6.283164044300404, -41.33714237083565, 81.34076887918835, -70.99343319450264)
NP = 4


def scaled_cos(theta, turns):
    t = theta * INV_TURN + turns
    s = 0.25 - jnp.abs(t - jnp.round(t))
    u = s * s
    p = SIN[3] * SCALE
    for q in SIN[2::-1]:
        p = p * u + q * SCALE
    return (s * p).astype(BF)


def kernel(
    order, in_hbm, targ_hbm, freq_hbm, w_hbm, e_hbm, phase_ref, eig_ref, tail_ref,
    we_v, g_v, ft_last, resid_last, coeff_last, res_v,
    x_v, freq_v, targ_v, scale_v, feat_v, ft_v,
    own_v, send_c, recv_c, buf_a, recv_a, own_b, buf_b, recv_b, recv_z,
    gath, rk_v,
    load_sem, sx, rx, sc, rc, sa, ra, sb, rb, sz, rz, sgb, rgb, sga, rga, sgc, rgc,
):
    f, c = lax.axis_index("feat"), lax.axis_index("rep")
    z, x, y = f // 16, (f // 4) % 4, f % 4

    def at_x(d):
        return (z * 16 + ((x + d) % 4) * 4 + y, c)

    def at_y(d):
        return (z * 16 + x * 4 + (y + d) % 4, c)

    def at_z(d):
        return (((z + d) % 8) * 16 + x * 4 + y, c)

    mate = (f, 1 - c)
    barrier = pltpu.get_barrier_semaphore()
    everyone = [mate]
    everyone += [at_x(d) for d in (1, 2, 3)] + [at_y(d) for d in (1, 2, 3)]
    everyone += [at_z(d) for d in range(1, 8)]
    for peer in everyone:
        pl.semaphore_signal(barrier, inc=1, device_id=peer, device_id_type=MESH)

    loads = [
        (in_hbm, x_v.at[0]),
        (freq_hbm, freq_v),
        (w_hbm, we_v.at[:, 0:512]),
        (e_hbm, we_v.at[:, 512:768]),
        (targ_hbm.at[:, 0:384], targ_v.at[0]),
        (targ_hbm.at[:, 384:512], targ_v.at[1, :, 0:128]),
    ]
    loads = [pltpu.make_async_copy(s, d, load_sem.at[i]) for i, (s, d) in enumerate(loads)]
    for load in loads:
        load.start()
    targ_v[1, :, 128:384] = jnp.zeros((512, 256), BF)
    scale_v[...] = jnp.ones_like(scale_v)
    scale_v[1, :, 128:384] = 1.0 - tail_ref[...] / eig_ref[...]

    def remote(src, dst, send, recv, peer):
        return pltpu.make_async_remote_copy(
            src_ref=src, dst_ref=dst, send_sem=send, recv_sem=recv,
            device_id=peer, device_id_type=MESH,
        )

    def first(p):
        return (x, at_x) if p % 2 == 0 else (y, at_y)

    def second(p):
        return (y, at_y) if p % 2 == 0 else (x, at_x)

    def core_copy(p):
        return remote(send_c.at[p], recv_c.at[p], sc.at[p], rc.at[p], mate)

    def a_copies(p):
        i, peer = first(p)
        return [
            remote(buf_a.at[p, pl.ds(((i + d) % 4) * 4, 4)], recv_a.at[p, d - 1], sa.at[p, d - 1], ra.at[p, d - 1], peer(d))
            for d in (1, 2, 3)
        ]

    def b_copies(p):
        i, peer = second(p)
        return [
            remote(buf_b.at[p, (i + d) % 4], recv_b.at[p, d - 1], sb.at[p, d - 1], rb.at[p, d - 1], peer(d))
            for d in (1, 2, 3)
        ]

    def z_copies(p):
        return [
            remote(recv_z.at[p, z], recv_z.at[p, z], sz.at[p, d - 1], rz.at[p, d - 1], at_z(d))
            for d in range(1, 8)
        ]

    def gb_copies(p):
        i, (k, peer) = first(p)[0], second(p)
        here = gath.at[p, 0, i * 4 + k]
        return [remote(here, here, sgb.at[p, d - 1], rgb.at[p, d - 1], peer(d)) for d in (1, 2, 3)]

    def ga_copies(p):
        i, peer = first(p)
        here = gath.at[p, 0, pl.ds(i * 4, 4)]
        return [remote(here, here, sga.at[p, d - 1], rga.at[p, d - 1], peer(d)) for d in (1, 2, 3)]

    def gc_copy(p):
        return remote(gath.at[p, 0], gath.at[p, 1], sgc.at[p], rgc.at[p], mate)

    def start(copies):
        for copy in copies:
            copy.start()

    def arrived(copies):
        for copy in copies:
            copy.wait_recv()

    def sent(copies):
        for copy in copies:
            copy.wait_send()

    def features(half, pair):
        def tile(n, carry):
            cols = pl.ds(pl.multiple_of(n * 1024, 1024), 1024)
            theta = lax.dot_general(
                x_v[half, :, pl.ds(pair * 256, 256)], freq_v[:, cols], (((0,), (0,)), ((), ())),
                preferred_element_type=F32,
            )
            value = scaled_cos(theta, phase_ref[:, cols] * INV_TURN)
            for q in (0, 1):
                feat_v[2 * pair + q, pl.ds(half * 128, 128), cols] = value[q * 128:(q + 1) * 128]
            return carry

        lax.fori_loop(0, 2, tile, 0)

    def project(p):
        def tile(n, carry):
            cols = pl.ds(pl.multiple_of(n * 256, 256), 256)
            part = jnp.dot(feat_v[p], we_v[:, cols], preferred_element_type=F32)
            own_v[p, :, cols] = part[0:128]
            send_c[p, :, cols] = part[128:256].astype(BF)
            return carry

        lax.fori_loop(0, 3, tile, 0)
        core_copy(p).start()

    def stage_1(p):
        arrived([core_copy(p)])
        for i in range(4):
            for j in range(2):
                rows = pl.ds(32 * i + 16 * j, 16)
                total = own_v[p, rows, :] + recv_c[p, rows, :].astype(F32)
                own_v[p, rows, :] = total
                for k in range(2):
                    buf_a[p, 4 * i + 2 * j + k] = total[:, 384 * k:384 * (k + 1)].astype(BF)
        start(a_copies(p))
        sent([core_copy(p)])

    def stage_2(p):
        arrived(a_copies(p))
        i = first(p)[0]
        for j in range(2):
            rows = pl.ds(pl.multiple_of(32 * i + 16 * j, 16), 16)
            for k in range(2):
                b = 2 * j + k
                total = own_v[p, rows, 384 * k:384 * (k + 1)]
                for d in range(3):
                    total = total + recv_a[p, d, b].astype(F32)
                own_b[p, b] = total
                buf_b[p, b] = total.astype(BF)
        start(b_copies(p))
        sent(a_copies(p))

    def stage_3(p):
        arrived(b_copies(p))
        k = second(p)[0]
        total = own_b[p, k]
        for d in range(3):
            total = total + recv_b[p, d].astype(F32)
        recv_z[p, z] = total.astype(BF)
        start(z_copies(p))
        sent(b_copies(p))

    def stage_4(p):
        arrived(z_copies(p))
        i, k = first(p)[0], second(p)[0]
        total = recv_z[p, 0].astype(F32)
        for d in range(1, 8):
            total = total + recv_z[p, d].astype(F32)
        rows = pl.ds(pl.multiple_of(p * 128 + 32 * i + 16 * (k // 2), 16), 16)
        total = total * scale_v[k % 2] - targ_v[k % 2, rows, :].astype(F32)
        gath[p, 0, i * 4 + k] = total.astype(BF)
        start(gb_copies(p))
        sent(z_copies(p))

    def stage_5(p):
        arrived(gb_copies(p))
        start(ga_copies(p))
        sent(gb_copies(p))

    def stage_6(p):
        arrived(ga_copies(p))
        gc_copy(p).start()
        sent(ga_copies(p))

    column = 4 * f + 2 * c

    def stage_7(p):
        arrived([gc_copy(p)])
        for half in range(2):
            for b in range(16):
                rows = half * 128 + 32 * (b // 4) + 16 * ((b % 4) // 2)
                rk_v[p, rows:rows + 16, 384 * (b % 2):384 * (b % 2 + 1)] = gath[p, half, b]
        sent([gc_copy(p)])
        pick = lax.broadcasted_iota(jnp.int32, (8, 512), 1) == lax.broadcasted_iota(jnp.int32, (8, 512), 0) + column
        pick = jnp.where(pick, 1.0, 0.0).astype(BF)
        shown = lax.dot_general(pick, rk_v[p, :, 0:512], (((1,), (1,)), ((), ())), preferred_element_type=F32)
        for half in range(2):
            res_v[half, :, p * 128:(p + 1) * 128] = shown[:, half * 128:(half + 1) * 128]
        resid = rk_v[p, :, 0:512]
        coeff = lax.dot_general(
            rk_v[p, :, 512:768], resid, (((0,), (0,)), ((), ())), preferred_element_type=F32
        )
        coeff = (-coeff).astype(BF)
        if p == NP - 1:
            resid_last[...] = resid
            coeff_last[...] = coeff
            return

        def tile(n, carry):
            rows = pl.ds(pl.multiple_of(n * 512, 512), 512)
            part = jnp.dot(ft_v[p, rows, :], resid, preferred_element_type=F32)
            part = part + jnp.dot(we_v[rows, 512:768], coeff, preferred_element_type=F32)
            if p > 0:
                part = part + g_v[rows, :]
            g_v[rows, :] = part
            return carry

        lax.fori_loop(0, 4, tile, 0)

    def flip(p):
        def tile(n, carry):
            cols = pl.ds(pl.multiple_of(n * 256, 256), 256)
            turned = feat_v[p, :, cols].T
            if p == NP - 1:
                ft_last[cols, :] = turned
            else:
                ft_v[p, cols, :] = turned
            return carry

        lax.fori_loop(0, 8, tile, 0)

    trade = remote(in_hbm, x_v.at[1], sx, rx, mate)

    def ready(n):
        for load in (loads[0:2], loads[2:])[n]:
            load.wait()

    def greet(n):
        pl.semaphore_wait(barrier, len(everyone))
        trade.start()

    steps = dict(
        L=ready, B=greet, T=lambda n: trade.wait(), F=lambda n: features(0, n), M=lambda n: features(1, n), P=project,
        X=flip, a=stage_1, b=stage_2, c=stage_3, d=stage_4, e=stage_5, f=stage_6, g=stage_7,
    )
    for op in " ".join(order).split():
        steps[op[0]](int(op[1:]))


def finish(we_v, g_v, ft_last, resid_last, coeff_last, shown_v, tail_ref, out_hbm, res_ref, out_v, store_sem):
    rate = 1.0 / tail_ref[...]

    def tile(n, carry):
        rows = pl.ds(pl.multiple_of(n * 512, 512), 512)
        part = jnp.dot(ft_last[rows, :], resid_last[...], preferred_element_type=F32)
        part = part + jnp.dot(we_v[rows, 512:768], coeff_last[...], preferred_element_type=F32)
        part = part + g_v[rows, :]
        out_v[rows, :] = (we_v[rows, 0:512].astype(F32) - part * rate).astype(BF)
        pltpu.make_async_copy(out_v.at[rows], out_hbm.at[rows], store_sem.at[n]).start()
        return carry

    lax.fori_loop(0, 4, tile, 0)
    c = lax.axis_index("rep")
    res_ref[:, pl.ds(pl.multiple_of(c * 512, 512), 512)] = shown_v[0, 0:2, :]
    res_ref[:, pl.ds(pl.multiple_of((1 - c) * 512, 512), 512)] = shown_v[1, 0:2, :]
    for n in range(4):
        rows = pl.ds(n * 512, 512)
        pltpu.make_async_copy(out_v.at[rows], out_hbm.at[rows], store_sem.at[n]).wait()


ORDER = (
    "L0 F0 B0 F1", "L1 T0 M0", "P0 P1 a0 M1", "a1 P2 P3 a2", "b0 a3 X0 b1", "X1 c0 b2 X2", "c1 b3 X3 d0",
    "c2 d1 c3 e0", "d2 e1 d3 f0", "e2 f1 e3 g0", "f2 g1 f3 g2", "g3",
)


def shards(inputs, targets, frequencies, phases, weights, eigvecs, eigvals, tail):
    hbm = pl.BlockSpec(memory_space=pl.ANY)
    vmem = pl.BlockSpec(memory_space=pltpu.VMEM)
    dma = pltpu.SemaphoreType.DMA
    chunk = (16, 384)
    tail = tail.reshape(1, 1)
    kept = pl.pallas_call(
        functools.partial(kernel, ORDER),
        out_shape=[
            pltpu.VMEM((2048, 768), BF),
            pltpu.VMEM((2048, 512), F32),
            pltpu.VMEM((2048, 256), BF),
            pltpu.VMEM((256, 512), BF),
            pltpu.VMEM((256, 512), BF),
            pltpu.VMEM((2, 8, 512), F32),
        ],
        in_specs=[hbm] * 5 + [vmem] * 3,
        out_specs=[vmem] * 6,
        scratch_shapes=[
            pltpu.VMEM((2, 440, 512), BF),
            pltpu.VMEM((440, 2048), BF),
            pltpu.VMEM((2, 512, 384), BF),
            pltpu.VMEM((2, 1, 384), F32),
            pltpu.VMEM((NP, 256, 2048), BF),
            pltpu.VMEM((NP - 1, 2048, 256), BF),
            pltpu.VMEM((NP, 128, 768), F32),
            pltpu.VMEM((NP, 128, 768), BF),
            pltpu.VMEM((NP, 128, 768), BF),
            pltpu.VMEM((NP, 16) + chunk, BF),
            pltpu.VMEM((NP, 3, 4) + chunk, BF),
            pltpu.VMEM((NP, 4) + chunk, F32),
            pltpu.VMEM((NP, 4) + chunk, BF),
            pltpu.VMEM((NP, 3) + chunk, BF),
            pltpu.VMEM((NP, 8) + chunk, BF),
            pltpu.VMEM((NP, 2, 16) + chunk, BF),
            pltpu.VMEM((NP, 256, 768), BF),
            dma((6,)),
            dma, dma,
            dma((NP,)), dma((NP,)),
            dma((NP, 3)), dma((NP, 3)),
            dma((NP, 3)), dma((NP, 3)),
            dma((NP, 7)), dma((NP, 7)),
            dma((NP, 3)), dma((NP, 3)),
            dma((NP, 3)), dma((NP, 3)),
            dma((NP,)), dma((NP,)),
        ],
        compiler_params=pltpu.CompilerParams(
            collective_id=0, has_side_effects=True, vmem_limit_bytes=48 << 20
        ),
        name="step",
    )(
        inputs.T, targets, frequencies, weights, eigvecs,
        phases.reshape(1, -1), eigvals.reshape(1, -1), tail,
    )
    new_weights, residual = pl.pallas_call(
        finish,
        out_shape=[jax.ShapeDtypeStruct((2048, 512), BF), jax.ShapeDtypeStruct((2, 1024), F32)],
        in_specs=[vmem] * 7,
        out_specs=[hbm, vmem],
        scratch_shapes=[pltpu.VMEM((2048, 512), BF), dma((4,))],
        compiler_params=pltpu.CompilerParams(vmem_limit_bytes=16 << 20),
        name="finish",
    )(*kept, tail)
    return (new_weights, residual.T)


def solution(mesh):
    in_specs = (
        P("rep", None),
        P("rep", None),
        P(None, ("feat", "rep")),
        P(("feat", "rep")),
        P(("feat", "rep"), None),
        P(("feat", "rep"), None),
        P(),
        P(),
    )
    out_specs = (P(("feat", "rep"), None), P(None, ("feat", "rep")))
    return jax.shard_map(shards, mesh=mesh, in_specs=in_specs, out_specs=out_specs, check_vma=False)
```

```python
import functools
import math

import jax
import jax.numpy as jnp
from jax import lax
from jax.experimental import pallas as pl
from jax.experimental.pallas import tpu as pltpu
from jax.sharding import PartitionSpec as P

MESH = pl.DeviceIdType.MESH
BF, F32 = jnp.bfloat16, jnp.float32
FEATURES = 524288
SCALE = math.sqrt(2.0 / FEATURES)
INV_TURN = 1.0 / (2.0 * math.pi)
SIN = (6.283164044300404, -41.33714237083565, 81.34076887918835, -70.99343319450264)
NP = 4


def scaled_cos(theta, turns):
    t = theta * INV_TURN + turns
    s = 0.25 - jnp.abs(t - jnp.round(t))
    u = s * s
    p = SIN[3] * SCALE
    for q in SIN[2::-1]:
        p = p * u + q * SCALE
    return (s * p).astype(BF)


def kernel(
    order, in_hbm, targ_hbm, freq_hbm, w_hbm, e_hbm, phase_hbm, eig_hbm, tail_hbm,
    we_v, g_v, ft_last, resid_last, coeff_last, res_v, rate_v,
    x_v, freq_v, targ_v, scale_v, feat_v, ft_v, coeff_v, phase_v, eig_v, tail_v,
    xt_v, own_v, send_c, recv_c, buf_a, recv_a, recv_z, gath, rk_v,
    load_sem, sx, rx, sc, rc, sa, ra, sz, rz, sg, rg, sgc, rgc,
):
    f, c = lax.axis_index("feat"), lax.axis_index("rep")
    z, x, y = f // 16, (f // 4) % 4, f % 4

    def in_plane(d):
        i, j = (x + d // 4) % 4, (y + d % 4) % 4
        return 4 * i + j, (z * 16 + 4 * i + j, c)

    def at_z(d):
        return (((z + d) % 8) * 16 + x * 4 + y, c)

    mate = (f, 1 - c)
    barrier = pltpu.get_barrier_semaphore()
    everyone = [mate] + [in_plane(d)[1] for d in range(1, 16)] + [at_z(d) for d in range(1, 8)]
    loads = [
        (in_hbm, x_v.at[0]),
        (phase_hbm, phase_v),
        (freq_hbm, freq_v),
        (w_hbm, we_v.at[:, 0:512]),
        (e_hbm, we_v.at[:, 512:768]),
        (eig_hbm, eig_v),
        (tail_hbm, tail_v),
        (targ_hbm.at[:, 0:384], targ_v.at[0]),
        (targ_hbm.at[:, 384:512], targ_v.at[1, :, 0:128]),
    ]
    loads = [pltpu.make_async_copy(s, d, load_sem.at[i]) for i, (s, d) in enumerate(loads)]
    for load in loads:
        load.start()
    for peer in everyone:
        pl.semaphore_signal(barrier, inc=1, device_id=peer, device_id_type=MESH)

    def remote(src, dst, send, recv, peer):
        return pltpu.make_async_remote_copy(
            src_ref=src, dst_ref=dst, send_sem=send, recv_sem=recv,
            device_id=peer, device_id_type=MESH,
        )

    slot = 4 * x + y

    def core_copy(p):
        return remote(send_c.at[p], recv_c.at[p], sc.at[p], rc.at[p], mate)

    def a_copies(p):
        copies = []
        for d in range(1, 16):
            there, peer = in_plane(d)
            copies.append(remote(buf_a.at[p, there], recv_a.at[p, d - 1], sa.at[p, d - 1], ra.at[p, d - 1], peer))
        return copies

    def z_copies(p):
        here = recv_z.at[p, z]
        return [remote(here, here, sz.at[p, d - 1], rz.at[p, d - 1], at_z(d)) for d in range(1, 8)]

    def g_copies(p):
        here = gath.at[p, 0, slot]
        return [remote(here, here, sg.at[p, d - 1], rg.at[p, d - 1], in_plane(d)[1]) for d in range(1, 16)]

    def gc_copy(p):
        return remote(gath.at[p, 0], gath.at[p, 1], sgc.at[p], rgc.at[p], mate)

    def start(copies):
        for copy in copies:
            copy.start()

    def arrived(copies):
        for copy in copies:
            copy.wait_recv()

    def sent(copies):
        for copy in copies:
            copy.wait_send()

    def turn_inputs(half):
        for i in range(4):
            xt_v[half, i * 128:(i + 1) * 128, :] = x_v[half, :, i * 128:(i + 1) * 128].T

    def features(half, rows):
        for n in range(4):
            cols = slice(n * 512, (n + 1) * 512)
            theta = jnp.dot(xt_v[half, rows, :], freq_v[:, cols], preferred_element_type=F32)
            feat_v[half, rows, cols] = scaled_cos(theta, phase_v[:, cols] * INV_TURN)

    def own_features(n):
        turn_inputs(0)
        features(0, slice(0, 512))

    def mate_features(p):
        features(1, slice(p * 128, (p + 1) * 128))

    def own_project(n):
        rows = slice(n * 256, (n + 1) * 256)
        own_v[rows, :] = jnp.dot(feat_v[0, rows, :], we_v[...], preferred_element_type=F32)

    def mate_project(p):
        part = jnp.dot(feat_v[1, p * 128:(p + 1) * 128, :], we_v[...], preferred_element_type=F32)
        send_c[p] = part.astype(BF)
        core_copy(p).start()

    def stage_core(p):
        arrived([core_copy(p)])
        for i in range(8):
            rows = pl.ds(16 * i, 16)
            here = pl.ds(128 * p + 16 * i, 16)
            total = own_v[here, :] + recv_c[p, rows, :].astype(F32)
            own_v[here, :] = total
            for k in range(2):
                buf_a[p, 2 * i + k] = total[:, 384 * k:384 * (k + 1)].astype(BF)
        start(a_copies(p))
        sent([core_copy(p)])

    def chunk(ref, first_row):
        rows = pl.ds(pl.multiple_of(first_row + 16 * (slot // 2), 16), 16)
        cols = pl.ds(pl.multiple_of(384 * (slot % 2), 128), 384)
        return ref[rows, cols]

    def stage_plane(p):
        arrived(a_copies(p))
        total = chunk(own_v, 128 * p)
        for d in range(15):
            total = total + recv_a[p, d].astype(F32)
        recv_z[p, z] = total.astype(BF)
        start(z_copies(p))
        sent(a_copies(p))

    def stage_line(p):
        arrived(z_copies(p))
        total = recv_z[p, 0].astype(F32)
        for d in range(1, 8):
            total = total + recv_z[p, d].astype(F32)
        rows = pl.ds(pl.multiple_of(p * 128 + 16 * (slot // 2), 16), 16)
        total = total * scale_v[slot % 2] - targ_v[slot % 2, rows, :].astype(F32)
        gath[p, 0, slot] = total.astype(BF)
        start(g_copies(p))
        sent(z_copies(p))

    def stage_gather(p):
        arrived(g_copies(p))
        gc_copy(p).start()
        sent(g_copies(p))

    column = 4 * f + 2 * c

    def stage_last(p):
        arrived([gc_copy(p)])
        for half in range(2):
            for b in range(16):
                rows = 256 * p + 128 * half + 16 * (b // 2)
                rk_v[rows:rows + 16, 384 * (b % 2):384 * (b % 2 + 1)] = gath[p, half, b]
        sent([gc_copy(p)])
        resid = rk_v[256 * p:256 * (p + 1), 0:512]
        pick = lax.broadcasted_iota(jnp.int32, (8, 512), 1) == lax.broadcasted_iota(jnp.int32, (8, 512), 0) + column
        pick = jnp.where(pick, 1.0, 0.0).astype(BF)
        shown = lax.dot_general(pick, resid, (((1,), (1,)), ((), ())), preferred_element_type=F32)
        for half in range(2):
            res_v[half, :, p * 128:(p + 1) * 128] = shown[:, half * 128:(half + 1) * 128]
        coeff = lax.dot_general(
            rk_v[256 * p:256 * (p + 1), 512:768], resid, (((0,), (0,)), ((), ())), preferred_element_type=F32
        )
        if p > 0:
            coeff = coeff + coeff_v[...]
        if p < NP - 1:
            coeff_v[...] = coeff
        else:
            coeff_last[...] = (-coeff).astype(BF)
            resid_last[...] = resid

    def gradient(n):
        depth = pl.ds(0, 512) if n == 0 else pl.ds(512, 256)

        def tile(i, carry):
            rows = pl.ds(pl.multiple_of(i * 512, 512), 512)
            part = jnp.dot(ft_v[rows, depth], rk_v[depth, 0:512], preferred_element_type=F32)
            g_v[rows, :] = part if n == 0 else part + g_v[rows, :]
            return carry

        lax.fori_loop(0, 4, tile, 0)

    def flip(p):
        def tile(n, carry):
            cols = pl.ds(pl.multiple_of(n * 256, 256), 256)
            for half in range(2):
                turned = feat_v[half, p * 128:(p + 1) * 128, cols].T
                if p == NP - 1:
                    ft_last[cols, half * 128:(half + 1) * 128] = turned
                else:
                    ft_v[cols, p * 256 + half * 128:p * 256 + (half + 1) * 128] = turned
            return carry

        lax.fori_loop(0, 8, tile, 0)

    trade = remote(in_hbm, x_v.at[1], sx, rx, mate)

    def ready(n):
        if n == 0:
            for load in loads[0:3]:
                load.wait()
            targ_v[1, :, 128:384] = jnp.zeros((512, 256), BF)
        else:
            for load in loads[3:]:
                load.wait()
            scale_v[...] = jnp.ones_like(scale_v)
            scale_v[1, :, 128:384] = 1.0 - tail_v[...] / eig_v[...]
            rate_v[...] = jnp.broadcast_to(1.0 / tail_v[...], (1, 512))

    def greet(n):
        pl.semaphore_wait(barrier, len(everyone))
        trade.start()

    def meet(n):
        trade.wait()
        turn_inputs(1)

    steps = dict(
        L=ready, B=greet, T=meet, F=own_features, O=own_project, M=mate_features, P=mate_project,
        X=flip, a=stage_core, b=stage_plane, d=stage_line, f=stage_gather, g=stage_last, G=gradient,
    )
    for op in " ".join(order).split():
        steps[op[0]](int(op[1:]))


def finish(
    we_v, g_v, ft_last, resid_last, coeff_last, shown_v, rate_v,
    out_hbm, res_hbm, out_v, res_v, store_sem,
):
    c = lax.axis_index("rep")
    res_v[:, pl.ds(pl.multiple_of(c * 512, 512), 512)] = shown_v[0, 0:2, :]
    res_v[:, pl.ds(pl.multiple_of((1 - c) * 512, 512), 512)] = shown_v[1, 0:2, :]
    show = pltpu.make_async_copy(res_v, res_hbm, store_sem.at[4])
    show.start()

    def tile(n, carry):
        rows = pl.ds(pl.multiple_of(n * 512, 512), 512)
        part = jnp.dot(ft_last[rows, :], resid_last[...], preferred_element_type=F32)
        part = part + jnp.dot(we_v[rows, 512:768], coeff_last[...], preferred_element_type=F32)
        part = part + g_v[rows, :]
        out_v[rows, :] = (we_v[rows, 0:512].astype(F32) - part * rate_v[...]).astype(BF)
        pltpu.make_async_copy(out_v.at[rows], out_hbm.at[rows], store_sem.at[n]).start()
        return carry

    lax.fori_loop(0, 4, tile, 0)
    for n in range(4):
        rows = pl.ds(n * 512, 512)
        pltpu.make_async_copy(out_v.at[rows], out_hbm.at[rows], store_sem.at[n]).wait()
    show.wait()


ORDER = (
    "L0 F0 B0 L1", "O0 T0 M0 P0", "O1 a0 M1 P1", "M2 P2 a1", "M3 P3 a2", "X0 a3 X1", "b0 X2 b1 X3", "b2 b3 d0 d1",
    "d2 d3 f0 f1", "g0 f2 g1 f3", "G0 g2 G1 g3",
)


def shards(inputs, targets, frequencies, phases, weights, eigvecs, eigvals, tail):
    hbm = pl.BlockSpec(memory_space=pl.ANY)
    vmem = pl.BlockSpec(memory_space=pltpu.VMEM)
    dma = pltpu.SemaphoreType.DMA
    chunk = (16, 384)
    kept = pl.pallas_call(
        functools.partial(kernel, ORDER),
        out_shape=[
            pltpu.VMEM((2048, 768), BF),
            pltpu.VMEM((2048, 512), F32),
            pltpu.VMEM((2048, 256), BF),
            pltpu.VMEM((256, 512), BF),
            pltpu.VMEM((256, 512), BF),
            pltpu.VMEM((2, 8, 512), F32),
            pltpu.VMEM((1, 512), F32),
        ],
        in_specs=[hbm] * 8,
        out_specs=[vmem] * 7,
        scratch_shapes=[
            pltpu.VMEM((2, 440, 512), BF),
            pltpu.VMEM((440, 2048), BF),
            pltpu.VMEM((2, 512, 384), BF),
            pltpu.VMEM((2, 1, 384), F32),
            pltpu.VMEM((2, 512, 2048), BF),
            pltpu.VMEM((2048, 768), BF),
            pltpu.VMEM((256, 512), F32),
            pltpu.VMEM((1, 2048), F32),
            pltpu.VMEM((1, 256), F32),
            pltpu.VMEM((1, 1), F32),
            pltpu.VMEM((2, 512, 440), BF),
            pltpu.VMEM((512, 768), F32),
            pltpu.VMEM((NP, 128, 768), BF),
            pltpu.VMEM((NP, 128, 768), BF),
            pltpu.VMEM((NP, 16) + chunk, BF),
            pltpu.VMEM((NP, 15) + chunk, BF),
            pltpu.VMEM((NP, 8) + chunk, BF),
            pltpu.VMEM((NP, 2, 16) + chunk, BF),
            pltpu.VMEM((1024, 768), BF),
            dma((9,)),
            dma, dma,
            dma((NP,)), dma((NP,)),
            dma((NP, 15)), dma((NP, 15)),
            dma((NP, 7)), dma((NP, 7)),
            dma((NP, 15)), dma((NP, 15)),
            dma((NP,)), dma((NP,)),
        ],
        compiler_params=pltpu.CompilerParams(
            collective_id=0, has_side_effects=True, vmem_limit_bytes=48 << 20
        ),
        name="step",
    )(
        inputs.T, targets, frequencies, weights, eigvecs,
        phases.reshape(1, -1), eigvals.reshape(1, -1), tail.reshape(1, 1),
    )
    new_weights, residual = pl.pallas_call(
        finish,
        out_shape=[jax.ShapeDtypeStruct((2048, 512), BF), jax.ShapeDtypeStruct((2, 1024), F32)],
        in_specs=[vmem] * 7,
        out_specs=[hbm, hbm],
        scratch_shapes=[pltpu.VMEM((2048, 512), BF), pltpu.VMEM((2, 1024), F32), dma((5,))],
        compiler_params=pltpu.CompilerParams(vmem_limit_bytes=16 << 20),
        name="finish",
    )(*kept)
    return (new_weights, residual.T)


def solution(mesh):
    in_specs = (
        P("rep", None),
        P("rep", None),
        P(None, ("feat", "rep")),
        P(("feat", "rep")),
        P(("feat", "rep"), None),
        P(("feat", "rep"), None),
        P(),
        P(),
    )
    out_specs = (P(("feat", "rep"), None), P(None, ("feat", "rep")))
    return jax.shard_map(shards, mesh=mesh, in_specs=in_specs, out_specs=out_specs, check_vma=False)
```

```python
import functools
import math

import jax
import jax.numpy as jnp
from jax import lax
from jax.experimental import pallas as pl
from jax.experimental.pallas import tpu as pltpu
from jax.sharding import PartitionSpec as P

MESH = pl.DeviceIdType.MESH
BF, F32 = jnp.bfloat16, jnp.float32
FEATURES = 524288
SCALE = math.sqrt(2.0 / FEATURES)
INV_TURN = 1.0 / (2.0 * math.pi)
SIN = (6.283164044300404, -41.33714237083565, 81.34076887918835, -70.99343319450264)
NP = 4


def scaled_cos(theta, turns):
    t = theta * INV_TURN + turns
    s = 0.25 - jnp.abs(t - jnp.round(t))
    u = s * s
    p = SIN[3] * SCALE
    for q in SIN[2::-1]:
        p = p * u + q * SCALE
    return (s * p).astype(BF)


def kernel(
    order, in_hbm, targ_hbm, freq_hbm, w_hbm, e_hbm, phase_hbm, eig_hbm, tail_hbm,
    we_v, g_v, ft_last, resid_last, coeff_last, res_v, rate_v,
    x_v, freq_v, targ_v, scale_v, feat_v, ft_v, coeff_v, phase_v, eig_v, tail_v,
    xt_v, own_v, send_c, recv_c, buf_a, recv_a, recv_z, gath, rk_v,
    load_sem, sx, rx, sc, rc, sa, ra, sz, rz, sg, rg, sgc, rgc,
):
    f, c = lax.axis_index("feat"), lax.axis_index("rep")
    z, x, y = f // 16, (f // 4) % 4, f % 4

    def in_plane(d):
        i, j = (x + d // 4) % 4, (y + d % 4) % 4
        return 4 * i + j, (z * 16 + 4 * i + j, c)

    def at_z(d):
        return (((z + d) % 8) * 16 + x * 4 + y, c)

    mate = (f, 1 - c)
    barrier = pltpu.get_barrier_semaphore()
    everyone = [mate] + [in_plane(d)[1] for d in range(1, 16)] + [at_z(d) for d in range(1, 8)]
    loads = [
        (in_hbm, x_v.at[0]),
        (phase_hbm, phase_v),
        (freq_hbm, freq_v),
        (w_hbm, we_v.at[:, 0:512]),
        (e_hbm, we_v.at[:, 512:768]),
        (eig_hbm, eig_v),
        (tail_hbm, tail_v),
        (targ_hbm.at[:, 0:384], targ_v.at[0]),
        (targ_hbm.at[:, 384:512], targ_v.at[1, :, 0:128]),
    ]
    loads = [pltpu.make_async_copy(s, d, load_sem.at[i]) for i, (s, d) in enumerate(loads)]
    for load in loads:
        load.start()
    for peer in everyone:
        pl.semaphore_signal(barrier, inc=1, device_id=peer, device_id_type=MESH)

    def remote(src, dst, send, recv, peer):
        return pltpu.make_async_remote_copy(
            src_ref=src, dst_ref=dst, send_sem=send, recv_sem=recv,
            device_id=peer, device_id_type=MESH,
        )

    slot = 4 * x + y

    def core_copy(p):
        return remote(send_c.at[p], recv_c.at[p], sc.at[p], rc.at[p], mate)

    def a_copies(p):
        copies = []
        for d in range(1, 16):
            there, peer = in_plane(d)
            copies.append(remote(buf_a.at[p, there], recv_a.at[p, d - 1], sa.at[p], ra.at[p], peer))
        return copies

    def z_copies(p):
        here = recv_z.at[p, z]
        return [remote(here, here, sz.at[p], rz.at[p], at_z(d)) for d in range(1, 8)]

    def g_copies(p):
        here = gath.at[p, 0, slot]
        return [remote(here, here, sg.at[p], rg.at[p], in_plane(d)[1]) for d in range(1, 16)]

    def a_all(p):
        return remote(recv_a.at[p], recv_a.at[p], sa.at[p], ra.at[p], mate)

    def z_all(p):
        here = recv_z.at[p, 0:7]
        return remote(here, here, sz.at[p], rz.at[p], mate)

    def g_all(p):
        here = gath.at[p, 0, 0:15]
        return remote(here, here, sg.at[p], rg.at[p], mate)

    def gc_copy(p):
        return remote(gath.at[p, 0], gath.at[p, 1], sgc.at[p], rgc.at[p], mate)

    def start(copies):
        for copy in copies:
            copy.start()

    def turn_inputs(half):
        for i in range(4):
            xt_v[half, i * 128:(i + 1) * 128, :] = x_v[half, :, i * 128:(i + 1) * 128].T

    def features(half, rows):
        for n in range(4):
            cols = slice(n * 512, (n + 1) * 512)
            theta = jnp.dot(xt_v[half, rows, :], freq_v[:, cols], preferred_element_type=F32)
            feat_v[half, rows, cols] = scaled_cos(theta, phase_v[:, cols] * INV_TURN)

    def own_features(n):
        turn_inputs(0)
        features(0, slice(0, 512))

    def mate_features(p):
        features(1, slice(p * 128, (p + 1) * 128))

    def own_project(n):
        rows = slice(n * 256, (n + 1) * 256)
        own_v[rows, :] = jnp.dot(feat_v[0, rows, :], we_v[...], preferred_element_type=F32)

    def mate_project(p):
        part = jnp.dot(feat_v[1, p * 128:(p + 1) * 128, :], we_v[...], preferred_element_type=F32)
        send_c[p] = part.astype(BF)
        core_copy(p).start()

    def stage_core(p):
        core_copy(p).wait_recv()
        for i in range(8):
            rows = pl.ds(16 * i, 16)
            here = pl.ds(128 * p + 16 * i, 16)
            total = own_v[here, :] + recv_c[p, rows, :].astype(F32)
            own_v[here, :] = total
            for k in range(2):
                buf_a[p, 2 * i + k] = total[:, 384 * k:384 * (k + 1)].astype(BF)
        start(a_copies(p))
        core_copy(p).wait_send()

    def chunk(ref, first_row):
        rows = pl.ds(pl.multiple_of(first_row + 16 * (slot // 2), 16), 16)
        cols = pl.ds(pl.multiple_of(384 * (slot % 2), 128), 384)
        return ref[rows, cols]

    def stage_plane(p):
        a_all(p).wait_recv()
        total = chunk(own_v, 128 * p)
        for d in range(15):
            total = total + recv_a[p, d].astype(F32)
        recv_z[p, z] = total.astype(BF)
        start(z_copies(p))
        a_all(p).wait_send()

    def stage_line(p):
        z_all(p).wait_recv()
        total = recv_z[p, 0].astype(F32)
        for d in range(1, 8):
            total = total + recv_z[p, d].astype(F32)
        rows = pl.ds(pl.multiple_of(p * 128 + 16 * (slot // 2), 16), 16)
        total = total * scale_v[slot % 2] - targ_v[slot % 2, rows, :].astype(F32)
        gath[p, 0, slot] = total.astype(BF)
        start(g_copies(p))
        z_all(p).wait_send()

    def stage_gather(p):
        g_all(p).wait_recv()
        gc_copy(p).start()
        g_all(p).wait_send()

    column = 4 * f + 2 * c

    def stage_last(p):
        gc_copy(p).wait_recv()
        for half in range(2):
            for b in range(16):
                rows = 256 * p + 128 * half + 16 * (b // 2)
                rk_v[rows:rows + 16, 384 * (b % 2):384 * (b % 2 + 1)] = gath[p, half, b]
        gc_copy(p).wait_send()
        resid = rk_v[256 * p:256 * (p + 1), 0:512]
        pick = lax.broadcasted_iota(jnp.int32, (8, 512), 1) == lax.broadcasted_iota(jnp.int32, (8, 512), 0) + column
        pick = jnp.where(pick, 1.0, 0.0).astype(BF)
        shown = lax.dot_general(pick, resid, (((1,), (1,)), ((), ())), preferred_element_type=F32)
        for half in range(2):
            res_v[half, :, p * 128:(p + 1) * 128] = shown[:, half * 128:(half + 1) * 128]
        coeff = lax.dot_general(
            rk_v[256 * p:256 * (p + 1), 512:768], resid, (((0,), (0,)), ((), ())), preferred_element_type=F32
        )
        if p > 0:
            coeff = coeff + coeff_v[...]
        if p < NP - 1:
            coeff_v[...] = coeff
        else:
            coeff_last[...] = (-coeff).astype(BF)
            resid_last[...] = resid

    def gradient(n):
        depth = pl.ds(0, 512) if n == 0 else pl.ds(512, 256)

        def tile(i, carry):
            rows = pl.ds(pl.multiple_of(i * 512, 512), 512)
            part = jnp.dot(ft_v[rows, depth], rk_v[depth, 0:512], preferred_element_type=F32)
            g_v[rows, :] = part if n == 0 else part + g_v[rows, :]
            return carry

        lax.fori_loop(0, 4, tile, 0)

    def flip(p):
        def tile(n, carry):
            cols = pl.ds(pl.multiple_of(n * 256, 256), 256)
            for half in range(2):
                turned = feat_v[half, p * 128:(p + 1) * 128, cols].T
                if p == NP - 1:
                    ft_last[cols, half * 128:(half + 1) * 128] = turned
                else:
                    ft_v[cols, p * 256 + half * 128:p * 256 + (half + 1) * 128] = turned
            return carry

        lax.fori_loop(0, 8, tile, 0)

    trade = remote(in_hbm, x_v.at[1], sx, rx, mate)

    def ready(n):
        if n == 0:
            for load in loads[0:3]:
                load.wait()
            targ_v[1, :, 128:384] = jnp.zeros((512, 256), BF)
        else:
            for load in loads[3:]:
                load.wait()
            scale_v[...] = jnp.ones_like(scale_v)
            scale_v[1, :, 128:384] = 1.0 - tail_v[0] / eig_v[...]
            rate_v[...] = 1.0 / jnp.full((1, 512), tail_v[0], F32)

    def greet(n):
        pl.semaphore_wait(barrier, len(everyone))
        trade.start()

    def meet(n):
        trade.wait()
        turn_inputs(1)

    steps = dict(
        L=ready, B=greet, T=meet, F=own_features, O=own_project, M=mate_features, P=mate_project,
        X=flip, a=stage_core, b=stage_plane, d=stage_line, f=stage_gather, g=stage_last, G=gradient,
    )
    for op in " ".join(order).split():
        steps[op[0]](int(op[1:]))


def finish(
    we_v, g_v, ft_last, resid_last, coeff_last, shown_v, rate_v,
    out_hbm, res_hbm, out_v, res_v, store_sem,
):
    c = lax.axis_index("rep")
    res_v[:, pl.ds(pl.multiple_of(c * 512, 512), 512)] = shown_v[0, 0:2, :]
    res_v[:, pl.ds(pl.multiple_of((1 - c) * 512, 512), 512)] = shown_v[1, 0:2, :]
    show = pltpu.make_async_copy(res_v, res_hbm, store_sem.at[4])
    show.start()

    def tile(n, carry):
        rows = pl.ds(pl.multiple_of(n * 512, 512), 512)
        part = jnp.dot(ft_last[rows, :], resid_last[...], preferred_element_type=F32)
        part = part + jnp.dot(we_v[rows, 512:768], coeff_last[...], preferred_element_type=F32)
        part = part + g_v[rows, :]
        out_v[rows, :] = (we_v[rows, 0:512].astype(F32) - part * rate_v[...]).astype(BF)
        pltpu.make_async_copy(out_v.at[rows], out_hbm.at[rows], store_sem.at[n]).start()
        return carry

    lax.fori_loop(0, 4, tile, 0)
    for n in range(4):
        rows = pl.ds(n * 512, 512)
        pltpu.make_async_copy(out_v.at[rows], out_hbm.at[rows], store_sem.at[n]).wait()
    show.wait()


ORDER = (
    "L0 F0 B0 L1", "O0 T0 M0 P0", "O1 a0 M1 P1", "M2 P2 a1", "M3 P3 a2", "X0 a3 X1", "b0 X2 b1 X3", "b2 b3 d0 d1",
    "d2 d3 f0 f1", "g0 f2 g1 f3", "G0 g2 G1 g3",
)


def shards(inputs, targets, frequencies, phases, weights, eigvecs, eigvals, tail):
    hbm = pl.BlockSpec(memory_space=pl.ANY)
    vmem = pl.BlockSpec(memory_space=pltpu.VMEM)
    dma = pltpu.SemaphoreType.DMA
    chunk = (16, 384)
    kept = pl.pallas_call(
        functools.partial(kernel, ORDER),
        out_shape=[
            pltpu.VMEM((2048, 768), BF),
            pltpu.VMEM((2048, 512), F32),
            pltpu.VMEM((2048, 256), BF),
            pltpu.VMEM((256, 512), BF),
            pltpu.VMEM((256, 512), BF),
            pltpu.VMEM((2, 8, 512), F32),
            pltpu.VMEM((1, 512), F32),
        ],
        in_specs=[hbm] * 8,
        out_specs=[vmem] * 7,
        scratch_shapes=[
            pltpu.VMEM((2, 440, 512), BF),
            pltpu.VMEM((440, 2048), BF),
            pltpu.VMEM((2, 512, 384), BF),
            pltpu.VMEM((2, 1, 384), F32),
            pltpu.VMEM((2, 512, 2048), BF),
            pltpu.VMEM((2048, 768), BF),
            pltpu.VMEM((256, 512), F32),
            pltpu.VMEM((1, 2048), F32),
            pltpu.VMEM((1, 256), F32),
            pltpu.SMEM((1,), F32),
            pltpu.VMEM((2, 512, 440), BF),
            pltpu.VMEM((512, 768), F32),
            pltpu.VMEM((NP, 128, 768), BF),
            pltpu.VMEM((NP, 128, 768), BF),
            pltpu.VMEM((NP, 16) + chunk, BF),
            pltpu.VMEM((NP, 15) + chunk, BF),
            pltpu.VMEM((NP, 8) + chunk, BF),
            pltpu.VMEM((NP, 2, 16) + chunk, BF),
            pltpu.VMEM((1024, 768), BF),
            dma((9,)),
            dma, dma,
            dma((NP,)), dma((NP,)),
            dma((NP,)), dma((NP,)),
            dma((NP,)), dma((NP,)),
            dma((NP,)), dma((NP,)),
            dma((NP,)), dma((NP,)),
        ],
        compiler_params=pltpu.CompilerParams(
            collective_id=0, has_side_effects=True, vmem_limit_bytes=48 << 20
        ),
        name="step",
    )(
        inputs.T, targets, frequencies, weights, eigvecs,
        phases.reshape(1, -1), eigvals.reshape(1, -1), tail,
    )
    new_weights, residual = pl.pallas_call(
        finish,
        out_shape=[jax.ShapeDtypeStruct((2048, 512), BF), jax.ShapeDtypeStruct((2, 1024), F32)],
        in_specs=[vmem] * 7,
        out_specs=[hbm, hbm],
        scratch_shapes=[pltpu.VMEM((2048, 512), BF), pltpu.VMEM((2, 1024), F32), dma((5,))],
        compiler_params=pltpu.CompilerParams(vmem_limit_bytes=16 << 20),
        name="finish",
    )(*kept)
    return (new_weights, residual.T)


def solution(mesh):
    in_specs = (
        P("rep", None),
        P("rep", None),
        P(None, ("feat", "rep")),
        P(("feat", "rep")),
        P(("feat", "rep"), None),
        P(("feat", "rep"), None),
        P(),
        P(),
    )
    out_specs = (P(("feat", "rep"), None), P(None, ("feat", "rep")))
    return jax.shard_map(shards, mesh=mesh, in_specs=in_specs, out_specs=out_specs, check_vma=False)
```

```python
import functools
import math

import jax
import jax.numpy as jnp
from jax import lax
from jax.experimental import pallas as pl
from jax.experimental.pallas import tpu as pltpu
from jax.sharding import PartitionSpec as P

MESH = pl.DeviceIdType.MESH
BF, F32 = jnp.bfloat16, jnp.float32
FEATURES = 524288
SCALE = math.sqrt(2.0 / FEATURES)
INV_TURN = 1.0 / (2.0 * math.pi)
SIN = (6.283164044300404, -41.33714237083565, 81.34076887918835, -70.99343319450264)
NP = 4


def scaled_cos(theta, turns):
    t = theta * INV_TURN + turns
    s = 0.25 - jnp.abs(t - jnp.round(t))
    u = s * s
    p = SIN[3] * SCALE
    for q in SIN[2::-1]:
        p = p * u + q * SCALE
    return (s * p).astype(BF)


def kernel(
    order, in_hbm, targ_hbm, freq_hbm, w_hbm, e_hbm, phase_hbm, eig_hbm, tail_hbm,
    w_v, ef_v, g_v, rc_last, res_v, rate_v,
    x_v, freq_v, targ_v, scale_v, feat_v, ft_v, coeff_v, phase_v, eig_v, tail_v,
    xt_v, own_v, send_c, recv_c, buf_a, recv_a, recv_z, gath, rk_v,
    load_sem, sx, rx, sc, rc, sa, ra, sz, rz, sg, rg, sgc, rgc,
):
    f, c = lax.axis_index("feat"), lax.axis_index("rep")
    z, x, y = f // 16, (f // 4) % 4, f % 4

    def in_plane(d):
        i, j = (x + d // 4) % 4, (y + d % 4) % 4
        return 4 * i + j, (z * 16 + 4 * i + j, c)

    def at_z(d):
        return (((z + d) % 8) * 16 + x * 4 + y, c)

    mate = (f, 1 - c)
    barrier = pltpu.get_barrier_semaphore()
    everyone = [mate] + [in_plane(d)[1] for d in range(1, 16)] + [at_z(d) for d in range(1, 8)]
    loads = [
        (in_hbm, x_v.at[0]),
        (phase_hbm, phase_v),
        (freq_hbm, freq_v),
        (w_hbm, w_v),
        (e_hbm, ef_v.at[:, 0:256]),
        (eig_hbm, eig_v),
        (tail_hbm, tail_v),
        (targ_hbm.at[:, 0:384], targ_v.at[0]),
        (targ_hbm.at[:, 384:512], targ_v.at[1, :, 0:128]),
    ]
    loads = [pltpu.make_async_copy(s, d, load_sem.at[i]) for i, (s, d) in enumerate(loads)]
    for load in loads:
        load.start()
    for peer in everyone:
        pl.semaphore_signal(barrier, inc=1, device_id=peer, device_id_type=MESH)

    def remote(src, dst, send, recv, peer):
        return pltpu.make_async_remote_copy(
            src_ref=src, dst_ref=dst, send_sem=send, recv_sem=recv,
            device_id=peer, device_id_type=MESH,
        )

    slot = 4 * x + y

    def core_copy(p):
        return remote(send_c.at[p], recv_c.at[p], sc.at[p], rc.at[p], mate)

    def a_copies(p):
        copies = []
        for d in range(1, 16):
            there, peer = in_plane(d)
            copies.append(remote(buf_a.at[p, there], recv_a.at[p, d - 1], sa.at[p], ra.at[p], peer))
        return copies

    def z_copies(p):
        here = recv_z.at[p, z]
        return [remote(here, here, sz.at[p], rz.at[p], at_z(d)) for d in range(1, 8)]

    def g_copies(p):
        here = gath.at[p, 0, slot]
        return [remote(here, here, sg.at[p], rg.at[p], in_plane(d)[1]) for d in range(1, 16)]

    def a_all(p):
        return remote(recv_a.at[p], recv_a.at[p], sa.at[p], ra.at[p], mate)

    def z_all(p):
        here = recv_z.at[p, 0:7]
        return remote(here, here, sz.at[p], rz.at[p], mate)

    def g_all(p):
        here = gath.at[p, 0, 0:15]
        return remote(here, here, sg.at[p], rg.at[p], mate)

    def gc_copy(p):
        return remote(gath.at[p, 0], gath.at[p, 1], sgc.at[p], rgc.at[p], mate)

    def start(copies):
        for copy in copies:
            copy.start()

    def turn_inputs(half):
        for i in range(4):
            xt_v[half, i * 128:(i + 1) * 128, :] = x_v[half, :, i * 128:(i + 1) * 128].T

    def features(half, rows):
        for n in range(4):
            cols = slice(n * 512, (n + 1) * 512)
            theta = jnp.dot(xt_v[half, rows, :], freq_v[:, cols], preferred_element_type=F32)
            feat_v[half, rows, cols] = scaled_cos(theta, phase_v[:, cols] * INV_TURN)

    def project(half, rows):
        feats = feat_v[half, rows, :]
        on_w = jnp.dot(feats, w_v[...], preferred_element_type=F32)
        return on_w, jnp.dot(feats, ef_v[:, 0:256], preferred_element_type=F32)

    def own_features(n):
        features(0, slice(0, 512))

    def own_project(n):
        rows = slice(n * 256, (n + 1) * 256)
        own_v[rows, 0:512], own_v[rows, 512:768] = project(0, rows)

    def mate_features(p):
        features(1, slice(p * 128, (p + 1) * 128))

    def mate_project(p):
        on_w, on_e = project(1, slice(p * 128, (p + 1) * 128))
        send_c[p, :, 0:512] = on_w.astype(BF)
        send_c[p, :, 512:768] = on_e.astype(BF)
        core_copy(p).start()

    def stage_core(p):
        core_copy(p).wait_recv()
        for i in range(8):
            rows = pl.ds(16 * i, 16)
            here = pl.ds(128 * p + 16 * i, 16)
            total = own_v[here, :] + recv_c[p, rows, :].astype(F32)
            own_v[here, :] = total
            for k in range(2):
                buf_a[p, 2 * i + k] = total[:, 384 * k:384 * (k + 1)].astype(BF)
        start(a_copies(p))
        core_copy(p).wait_send()

    def chunk(ref, first_row):
        rows = pl.ds(pl.multiple_of(first_row + 16 * (slot // 2), 16), 16)
        cols = pl.ds(pl.multiple_of(384 * (slot % 2), 128), 384)
        return ref[rows, cols]

    def stage_plane(p):
        a_all(p).wait_recv()
        total = chunk(own_v, 128 * p)
        for d in range(15):
            total = total + recv_a[p, d].astype(F32)
        recv_z[p, z] = total.astype(BF)
        start(z_copies(p))
        a_all(p).wait_send()

    def stage_line(p):
        z_all(p).wait_recv()
        total = recv_z[p, 0].astype(F32)
        for d in range(1, 8):
            total = total + recv_z[p, d].astype(F32)
        rows = pl.ds(pl.multiple_of(p * 128 + 16 * (slot // 2), 16), 16)
        total = total * scale_v[slot % 2] - targ_v[slot % 2, rows, :].astype(F32)
        gath[p, 0, slot] = total.astype(BF)
        start(g_copies(p))
        z_all(p).wait_send()

    def stage_gather(p):
        g_all(p).wait_recv()
        gc_copy(p).start()
        g_all(p).wait_send()

    column = 4 * f + 2 * c

    def stage_last(p):
        gc_copy(p).wait_recv()
        for half in range(2):
            for b in range(16):
                rows = 256 * p + 128 * half + 16 * (b // 2)
                rk_v[rows:rows + 16, 384 * (b % 2):384 * (b % 2 + 1)] = gath[p, half, b]
        gc_copy(p).wait_send()
        resid = rk_v[256 * p:256 * (p + 1), 0:512]
        pick = lax.broadcasted_iota(jnp.int32, (8, 512), 1) == lax.broadcasted_iota(jnp.int32, (8, 512), 0) + column
        pick = jnp.where(pick, 1.0, 0.0).astype(BF)
        shown = lax.dot_general(pick, resid, (((1,), (1,)), ((), ())), preferred_element_type=F32)
        for half in range(2):
            res_v[half, :, p * 128:(p + 1) * 128] = shown[:, half * 128:(half + 1) * 128]
        coeff = lax.dot_general(
            rk_v[256 * p:256 * (p + 1), 512:768], resid, (((0,), (0,)), ((), ())), preferred_element_type=F32
        )
        if p > 0:
            coeff = coeff + coeff_v[...]
        if p < NP - 1:
            coeff_v[...] = coeff
        else:
            rc_last[0:256, :] = (-coeff).astype(BF)
            rc_last[256:512, :] = resid

    def gradient(n):
        depth = pl.ds(0, 256) if n == 0 else pl.ds(256, 512)

        def tile(i, carry):
            rows = pl.ds(pl.multiple_of(i * 512, 512), 512)
            part = jnp.dot(ft_v[rows, depth], rk_v[depth, 0:512], preferred_element_type=F32)
            g_v[rows, :] = part if n == 0 else part + g_v[rows, :]
            return carry

        lax.fori_loop(0, 4, tile, 0)

    def flip(p):
        def tile(n, carry):
            cols = pl.ds(pl.multiple_of(n * 256, 256), 256)
            for half in range(2):
                turned = feat_v[half, p * 128:(p + 1) * 128, cols].T
                if p == NP - 1:
                    ef_v[cols, 256 + half * 128:256 + (half + 1) * 128] = turned
                else:
                    ft_v[cols, p * 256 + half * 128:p * 256 + (half + 1) * 128] = turned
            return carry

        lax.fori_loop(0, 8, tile, 0)

    trade = remote(in_hbm, x_v.at[1], sx, rx, mate)

    def ready(n):
        if n == 0:
            for load in loads[0:3]:
                load.wait()
            turn_inputs(0)
            targ_v[1, :, 128:384] = jnp.zeros((512, 256), BF)
        else:
            for load in loads[3:]:
                load.wait()
            scale_v[...] = jnp.ones_like(scale_v)
            scale_v[1, :, 128:384] = 1.0 - tail_v[0] / eig_v[...]
            rate_v[...] = 1.0 / jnp.full((1, 512), tail_v[0], F32)

    def greet(n):
        pl.semaphore_wait(barrier, len(everyone))
        trade.start()

    def meet(n):
        trade.wait()
        turn_inputs(1)

    steps = dict(
        L=ready, B=greet, T=meet, F=own_features, O=own_project, M=mate_features, P=mate_project,
        X=flip, a=stage_core, b=stage_plane, d=stage_line, f=stage_gather, g=stage_last, G=gradient,
    )
    for op in " ".join(order).split():
        steps[op[0]](int(op[1:]))


def finish(
    w_v, ef_v, g_v, rc_last, shown_v, rate_v,
    out_hbm, res_hbm, out_v, res_v, store_sem,
):
    c = lax.axis_index("rep")
    res_v[:, pl.ds(pl.multiple_of(c * 512, 512), 512)] = shown_v[0, 0:2, :]
    res_v[:, pl.ds(pl.multiple_of((1 - c) * 512, 512), 512)] = shown_v[1, 0:2, :]
    show = pltpu.make_async_copy(res_v, res_hbm, store_sem.at[4])
    show.start()

    def tile(n, carry):
        rows = pl.ds(pl.multiple_of(n * 512, 512), 512)
        part = jnp.dot(ef_v[rows, :], rc_last[...], preferred_element_type=F32) + g_v[rows, :]
        out_v[rows, :] = (w_v[rows, :].astype(F32) - part * rate_v[...]).astype(BF)
        pltpu.make_async_copy(out_v.at[rows], out_hbm.at[rows], store_sem.at[n]).start()
        return carry

    lax.fori_loop(0, 4, tile, 0)
    for n in range(4):
        rows = pl.ds(n * 512, 512)
        pltpu.make_async_copy(out_v.at[rows], out_hbm.at[rows], store_sem.at[n]).wait()
    show.wait()


ORDER = (
    "L0 L1 B0", "F0 O0 T0", "M0 P0 O1", "M1 P1 a0", "M2 P2 a1", "M3 P3 a2", "a3 X0 X1", "b0 X2 b1 X3", "b2 b3",
    "d0 d1 d2 d3", "f0 f1 g0 G0", "f2 g1 f3 g2", "G1 g3",
)


def shards(inputs, targets, frequencies, phases, weights, eigvecs, eigvals, tail):
    hbm = pl.BlockSpec(memory_space=pl.ANY)
    vmem = pl.BlockSpec(memory_space=pltpu.VMEM)
    dma = pltpu.SemaphoreType.DMA
    chunk = (16, 384)
    kept = pl.pallas_call(
        functools.partial(kernel, ORDER),
        out_shape=[
            pltpu.VMEM((2048, 512), BF),
            pltpu.VMEM((2048, 512), BF),
            pltpu.VMEM((2048, 512), F32),
            pltpu.VMEM((512, 512), BF),
            pltpu.VMEM((2, 8, 512), F32),
            pltpu.VMEM((1, 512), F32),
        ],
        in_specs=[hbm] * 8,
        out_specs=[vmem] * 6,
        scratch_shapes=[
            pltpu.VMEM((2, 440, 512), BF),
            pltpu.VMEM((440, 2048), BF),
            pltpu.VMEM((2, 512, 384), BF),
            pltpu.VMEM((2, 1, 384), F32),
            pltpu.VMEM((2, 512, 2048), BF),
            pltpu.VMEM((2048, 768), BF),
            pltpu.VMEM((256, 512), F32),
            pltpu.VMEM((1, 2048), F32),
            pltpu.VMEM((1, 256), F32),
            pltpu.SMEM((1,), F32),
            pltpu.VMEM((2, 512, 440), BF),
            pltpu.VMEM((512, 768), F32),
            pltpu.VMEM((NP, 128, 768), BF),
            pltpu.VMEM((NP, 128, 768), BF),
            pltpu.VMEM((NP, 16) + chunk, BF),
            pltpu.VMEM((NP, 15) + chunk, BF),
            pltpu.VMEM((NP, 8) + chunk, BF),
            pltpu.VMEM((NP, 2, 16) + chunk, BF),
            pltpu.VMEM((1024, 768), BF),
            dma((9,)),
            dma, dma,
            dma((NP,)), dma((NP,)),
            dma((NP,)), dma((NP,)),
            dma((NP,)), dma((NP,)),
            dma((NP,)), dma((NP,)),
            dma((NP,)), dma((NP,)),
        ],
        compiler_params=pltpu.CompilerParams(
            collective_id=0, has_side_effects=True, vmem_limit_bytes=48 << 20
        ),
        name="step",
    )(
        inputs.T, targets, frequencies, weights, eigvecs,
        phases.reshape(1, -1), eigvals.reshape(1, -1), tail,
    )
    new_weights, residual = pl.pallas_call(
        finish,
        out_shape=[jax.ShapeDtypeStruct((2048, 512), BF), jax.ShapeDtypeStruct((2, 1024), F32)],
        in_specs=[vmem] * 6,
        out_specs=[hbm, hbm],
        scratch_shapes=[pltpu.VMEM((2048, 512), BF), pltpu.VMEM((2, 1024), F32), dma((5,))],
        compiler_params=pltpu.CompilerParams(vmem_limit_bytes=16 << 20),
        name="finish",
    )(*kept)
    return (new_weights, residual.T)


def solution(mesh):
    in_specs = (
        P("rep", None),
        P("rep", None),
        P(None, ("feat", "rep")),
        P(("feat", "rep")),
        P(("feat", "rep"), None),
        P(("feat", "rep"), None),
        P(),
        P(),
    )
    out_specs = (P(("feat", "rep"), None), P(None, ("feat", "rep")))
    return jax.shard_map(shards, mesh=mesh, in_specs=in_specs, out_specs=out_specs, check_vma=False)
```

```python
import functools
import math

import jax
import jax.numpy as jnp
from jax import lax
from jax.experimental import pallas as pl
from jax.experimental.pallas import tpu as pltpu
from jax.sharding import PartitionSpec as P

MESH = pl.DeviceIdType.MESH
BF, F32 = jnp.bfloat16, jnp.float32
FEATURES = 524288
SCALE = math.sqrt(2.0 / FEATURES)
INV_TURN = 1.0 / (2.0 * math.pi)
SIN = (6.283164044300404, -41.33714237083565, 81.34076887918835, -70.99343319450264)
NP = 4


def scaled_cos(theta, turns):
    t = theta * INV_TURN + turns
    s = 0.25 - jnp.abs(t - jnp.round(t))
    u = s * s
    p = SIN[3] * SCALE
    for q in SIN[2::-1]:
        p = p * u + q * SCALE
    return (s * p).astype(BF)


def kernel(
    order, in_hbm, targ_hbm, freq_hbm, w_hbm, e_hbm, phase_hbm, eig_hbm, tail_hbm,
    w_v, ef_v, g_v, rc_last, res_v, rate_v,
    x_v, freq_v, targ_v, scale_v, feat_v, ft_v, coeff_v, phase_v, eig_v, tail_v,
    xt_v, own_v, send_c, recv_c, buf_a, recv_a, recv_z, gath, rk_v,
    load_sem, sx, rx, sc, rc, sa, ra, sz, rz, sg, rg, sgc, rgc,
):
    f, c = lax.axis_index("feat"), lax.axis_index("rep")
    z, x, y = f // 16, (f // 4) % 4, f % 4

    def in_plane(d):
        i, j = (x + d // 4) % 4, (y + d % 4) % 4
        return 4 * i + j, (z * 16 + 4 * i + j, c)

    def at_z(d):
        return (((z + d) % 8) * 16 + x * 4 + y, c)

    mate = (f, 1 - c)
    barrier = pltpu.get_barrier_semaphore()
    everyone = [mate] + [in_plane(d)[1] for d in range(1, 16)] + [at_z(d) for d in range(1, 8)]
    loads = [
        (in_hbm, x_v.at[0]),
        (phase_hbm, phase_v),
        (freq_hbm, freq_v),
        (w_hbm, w_v),
        (e_hbm, ef_v.at[:, 0:256]),
        (eig_hbm, eig_v),
        (tail_hbm, tail_v),
        (targ_hbm.at[:, 0:384], targ_v.at[0]),
        (targ_hbm.at[:, 384:512], targ_v.at[1, :, 0:128]),
    ]
    loads = [pltpu.make_async_copy(s, d, load_sem.at[i]) for i, (s, d) in enumerate(loads)]
    for load in loads:
        load.start()
    for peer in everyone:
        pl.semaphore_signal(barrier, inc=1, device_id=peer, device_id_type=MESH)

    def remote(src, dst, send, recv, peer):
        return pltpu.make_async_remote_copy(
            src_ref=src, dst_ref=dst, send_sem=send, recv_sem=recv,
            device_id=peer, device_id_type=MESH,
        )

    slot = 4 * x + y

    def core_copy(p):
        return remote(send_c.at[p], recv_c.at[p], sc.at[p], rc.at[p], mate)

    def a_copies(p):
        copies = []
        for d in range(1, 16):
            there, peer = in_plane(d)
            copies.append(remote(buf_a.at[p, there], recv_a.at[p, d - 1], sa.at[p], ra.at[p], peer))
        return copies

    def z_copies(p):
        here = recv_z.at[p, z]
        return [remote(here, here, sz.at[p], rz.at[p], at_z(d)) for d in range(1, 8)]

    def g_copies(p):
        here = gath.at[p, 0, slot]
        return [remote(here, here, sg.at[p], rg.at[p], in_plane(d)[1]) for d in range(1, 16)]

    def a_all(p):
        return remote(recv_a.at[p], recv_a.at[p], sa.at[p], ra.at[p], mate)

    def z_all(p):
        here = recv_z.at[p, 0:7]
        return remote(here, here, sz.at[p], rz.at[p], mate)

    def g_all(p):
        here = gath.at[p, 0, 0:15]
        return remote(here, here, sg.at[p], rg.at[p], mate)

    def gc_copy(p):
        return remote(gath.at[p, 0], gath.at[p, 1], sgc.at[p], rgc.at[p], mate)

    def start(copies):
        for copy in copies:
            copy.start()

    def turn_inputs(half):
        for i in range(4):
            xt_v[half, i * 128:(i + 1) * 128, :] = x_v[half, :, i * 128:(i + 1) * 128].T

    def features(half, rows):
        for n in range(4):
            cols = slice(n * 512, (n + 1) * 512)
            theta = jnp.dot(xt_v[half, rows, :], freq_v[:, cols], preferred_element_type=F32)
            feat_v[half, rows, cols] = scaled_cos(theta, phase_v[:, cols] * INV_TURN)

    def project(half, rows):
        feats = feat_v[half, rows, :]
        on_w = jnp.dot(feats, w_v[...], preferred_element_type=F32)
        return on_w, jnp.dot(feats, ef_v[:, 0:256], preferred_element_type=F32)

    def own_features(n):
        features(0, slice(0, 512))

    def own_project(n):
        rows = slice(n * 256, (n + 1) * 256)
        own_v[rows, 0:512], own_v[rows, 512:768] = project(0, rows)

    def mate_features(p):
        features(1, slice(p * 128, (p + 1) * 128))

    def mate_project(p):
        on_w, on_e = project(1, slice(p * 128, (p + 1) * 128))
        send_c[p, :, 0:512] = on_w.astype(BF)
        send_c[p, :, 512:768] = on_e.astype(BF)
        core_copy(p).start()

    def stage_core(p):
        core_copy(p).wait_recv()
        for i in range(8):
            rows = pl.ds(16 * i, 16)
            here = pl.ds(128 * p + 16 * i, 16)
            total = own_v[here, :] + recv_c[p, rows, :].astype(F32)
            own_v[here, :] = total
            for k in range(2):
                buf_a[p, 2 * i + k] = total[:, 384 * k:384 * (k + 1)].astype(BF)
        start(a_copies(p))
        core_copy(p).wait_send()

    def chunk(ref, first_row):
        rows = pl.ds(pl.multiple_of(first_row + 16 * (slot // 2), 16), 16)
        cols = pl.ds(pl.multiple_of(384 * (slot % 2), 128), 384)
        return ref[rows, cols]

    def stage_plane(p):
        a_all(p).wait_recv()
        total = chunk(own_v, 128 * p)
        for d in range(15):
            total = total + recv_a[p, d].astype(F32)
        recv_z[p, z] = total.astype(BF)
        start(z_copies(p))
        a_all(p).wait_send()

    def stage_line(p):
        z_all(p).wait_recv()
        total = recv_z[p, 0].astype(F32)
        for d in range(1, 8):
            total = total + recv_z[p, d].astype(F32)
        rows = pl.ds(pl.multiple_of(p * 128 + 16 * (slot // 2), 16), 16)
        total = total * scale_v[slot % 2] - targ_v[slot % 2, rows, :].astype(F32)
        gath[p, 0, slot] = total.astype(BF)
        start(g_copies(p))
        z_all(p).wait_send()

    def stage_gather(p):
        g_all(p).wait_recv()
        gc_copy(p).start()
        g_all(p).wait_send()

    column = 4 * f + 2 * c

    def stage_last(p):
        gc_copy(p).wait_recv()
        for half in range(2):
            for b in range(16):
                rows = 256 * p + 128 * half + 16 * (b // 2)
                rk_v[rows:rows + 16, 384 * (b % 2):384 * (b % 2 + 1)] = gath[p, half, b]
        gc_copy(p).wait_send()
        resid = rk_v[256 * p:256 * (p + 1), 0:512]
        pick = lax.broadcasted_iota(jnp.int32, (8, 512), 1) == lax.broadcasted_iota(jnp.int32, (8, 512), 0) + column
        pick = jnp.where(pick, 1.0, 0.0).astype(BF)
        shown = lax.dot_general(pick, resid, (((1,), (1,)), ((), ())), preferred_element_type=F32)
        for half in range(2):
            res_v[half, :, p * 128:(p + 1) * 128] = shown[:, half * 128:(half + 1) * 128]
        coeff = lax.dot_general(
            rk_v[256 * p:256 * (p + 1), 512:768], resid, (((0,), (0,)), ((), ())), preferred_element_type=F32
        )
        if p > 0:
            coeff = coeff + coeff_v[...]
        if p < NP - 1:
            coeff_v[...] = coeff
        else:
            rc_last[0:256, :] = (-coeff).astype(BF)
            rc_last[256:768, :] = rk_v[512:1024, 0:512]

    def gradient(n):
        def tile(i, carry):
            rows = pl.ds(pl.multiple_of(i * 512, 512), 512)
            g_v[rows, :] = jnp.dot(ft_v[rows, :], rk_v[0:512, 0:512], preferred_element_type=F32)
            return carry

        lax.fori_loop(0, 4, tile, 0)

    def flip(p):
        def tile(n, carry):
            cols = pl.ds(pl.multiple_of(n * 256, 256), 256)
            for half in range(2):
                turned = feat_v[half, p * 128:(p + 1) * 128, cols].T
                if p < 2:
                    ft_v[cols, p * 256 + half * 128:p * 256 + (half + 1) * 128] = turned
                else:
                    ef_v[cols, (p - 1) * 256 + half * 128:(p - 1) * 256 + (half + 1) * 128] = turned
            return carry

        lax.fori_loop(0, 8, tile, 0)

    trade = remote(in_hbm, x_v.at[1], sx, rx, mate)

    def ready(n):
        if n == 0:
            for load in loads[0:3]:
                load.wait()
            turn_inputs(0)
            targ_v[1, :, 128:384] = jnp.zeros((512, 256), BF)
        else:
            for load in loads[3:]:
                load.wait()
            scale_v[...] = jnp.ones_like(scale_v)
            scale_v[1, :, 128:384] = 1.0 - tail_v[0] / eig_v[...]
            rate_v[...] = 1.0 / jnp.full((1, 512), tail_v[0], F32)

    def greet(n):
        pl.semaphore_wait(barrier, len(everyone))
        trade.start()

    def meet(n):
        trade.wait()
        turn_inputs(1)

    steps = dict(
        L=ready, B=greet, T=meet, F=own_features, O=own_project, M=mate_features, P=mate_project,
        X=flip, a=stage_core, b=stage_plane, d=stage_line, f=stage_gather, g=stage_last, G=gradient,
    )
    for op in " ".join(order).split():
        steps[op[0]](int(op[1:]))


def finish(
    w_v, ef_v, g_v, rc_last, shown_v, rate_v,
    out_hbm, res_hbm, out_v, res_v, store_sem,
):
    c = lax.axis_index("rep")
    res_v[:, pl.ds(pl.multiple_of(c * 512, 512), 512)] = shown_v[0, 0:2, :]
    res_v[:, pl.ds(pl.multiple_of((1 - c) * 512, 512), 512)] = shown_v[1, 0:2, :]
    show = pltpu.make_async_copy(res_v, res_hbm, store_sem.at[4])
    show.start()

    def tile(n, carry):
        rows = pl.ds(pl.multiple_of(n * 512, 512), 512)
        part = jnp.dot(ef_v[rows, :], rc_last[...], preferred_element_type=F32) + g_v[rows, :]
        out_v[rows, :] = (w_v[rows, :].astype(F32) - part * rate_v[...]).astype(BF)
        pltpu.make_async_copy(out_v.at[rows], out_hbm.at[rows], store_sem.at[n]).start()
        return carry

    lax.fori_loop(0, 4, tile, 0)
    for n in range(4):
        rows = pl.ds(n * 512, 512)
        pltpu.make_async_copy(out_v.at[rows], out_hbm.at[rows], store_sem.at[n]).wait()
    show.wait()


ORDER = (
    "L0 F0 B0 L1", "O0 T0 M0 P0", "O1 a0 M1 P1", "M2 P2 a1", "M3 P3 a2", "X0 a3 X1", "b0 X2 b1 X3", "b2 b3",
    "d0 d1 d2 d3", "f0 f1 g0", "f2 g1 G0", "f3 g2 g3",
)


def shards(inputs, targets, frequencies, phases, weights, eigvecs, eigvals, tail):
    hbm = pl.BlockSpec(memory_space=pl.ANY)
    vmem = pl.BlockSpec(memory_space=pltpu.VMEM)
    dma = pltpu.SemaphoreType.DMA
    chunk = (16, 384)
    kept = pl.pallas_call(
        functools.partial(kernel, ORDER),
        out_shape=[
            pltpu.VMEM((2048, 512), BF),
            pltpu.VMEM((2048, 768), BF),
            pltpu.VMEM((2048, 512), F32),
            pltpu.VMEM((768, 512), BF),
            pltpu.VMEM((2, 8, 512), F32),
            pltpu.VMEM((1, 512), F32),
        ],
        in_specs=[hbm] * 8,
        out_specs=[vmem] * 6,
        scratch_shapes=[
            pltpu.VMEM((2, 440, 512), BF),
            pltpu.VMEM((440, 2048), BF),
            pltpu.VMEM((2, 512, 384), BF),
            pltpu.VMEM((2, 1, 384), F32),
            pltpu.VMEM((2, 512, 2048), BF),
            pltpu.VMEM((2048, 512), BF),
            pltpu.VMEM((256, 512), F32),
            pltpu.VMEM((1, 2048), F32),
            pltpu.VMEM((1, 256), F32),
            pltpu.SMEM((1,), F32),
            pltpu.VMEM((2, 512, 440), BF),
            pltpu.VMEM((512, 768), F32),
            pltpu.VMEM((NP, 128, 768), BF),
            pltpu.VMEM((NP, 128, 768), BF),
            pltpu.VMEM((NP, 16) + chunk, BF),
            pltpu.VMEM((NP, 15) + chunk, BF),
            pltpu.VMEM((NP, 8) + chunk, BF),
            pltpu.VMEM((NP, 2, 16) + chunk, BF),
            pltpu.VMEM((1024, 768), BF),
            dma((9,)),
            dma, dma,
            dma((NP,)), dma((NP,)),
            dma((NP,)), dma((NP,)),
            dma((NP,)), dma((NP,)),
            dma((NP,)), dma((NP,)),
            dma((NP,)), dma((NP,)),
        ],
        compiler_params=pltpu.CompilerParams(
            collective_id=0, has_side_effects=True, vmem_limit_bytes=48 << 20
        ),
        name="step",
    )(
        inputs.T, targets, frequencies, weights, eigvecs,
        phases.reshape(1, -1), eigvals.reshape(1, -1), tail,
    )
    new_weights, residual = pl.pallas_call(
        finish,
        out_shape=[jax.ShapeDtypeStruct((2048, 512), BF), jax.ShapeDtypeStruct((2, 1024), F32)],
        in_specs=[vmem] * 6,
        out_specs=[hbm, hbm],
        scratch_shapes=[pltpu.VMEM((2048, 512), BF), pltpu.VMEM((2, 1024), F32), dma((5,))],
        compiler_params=pltpu.CompilerParams(vmem_limit_bytes=16 << 20),
        name="finish",
    )(*kept)
    return (new_weights, residual.T)


def solution(mesh):
    in_specs = (
        P("rep", None),
        P("rep", None),
        P(None, ("feat", "rep")),
        P(("feat", "rep")),
        P(("feat", "rep"), None),
        P(("feat", "rep"), None),
        P(),
        P(),
    )
    out_specs = (P(("feat", "rep"), None), P(None, ("feat", "rep")))
    return jax.shard_map(shards, mesh=mesh, in_specs=in_specs, out_specs=out_specs, check_vma=False)
```

```python
import functools
import math

import jax
import jax.numpy as jnp
from jax import lax
from jax.experimental import pallas as pl
from jax.experimental.pallas import tpu as pltpu
from jax.sharding import PartitionSpec as P

MESH = pl.DeviceIdType.MESH
BF, F32 = jnp.bfloat16, jnp.float32
FEATURES = 524288
SCALE = math.sqrt(2.0 / FEATURES)
INV_TURN = 1.0 / (2.0 * math.pi)
SIN = (6.283164044300404, -41.33714237083565, 81.34076887918835, -70.99343319450264)
NP = 4


def scaled_cos(theta, turns):
    t = theta * INV_TURN + turns
    s = 0.25 - jnp.abs(t - jnp.round(t))
    u = s * s
    p = SIN[3] * SCALE
    for q in SIN[2::-1]:
        p = p * u + q * SCALE
    return (s * p).astype(BF)


def kernel(
    order, in_hbm, targ_hbm, freq_hbm, w_hbm, e_hbm, phase_hbm, eig_hbm, tail_hbm,
    w_v, ef_v, g_v, rc_last, res_v, rate_v,
    x_v, freq_v, targ_v, scale_v, feat_v, ft_v, coeff_v, phase_v, eig_v, tail_v,
    xt_v, own_v, send_c, recv_c, buf_a, recv_a, recv_z, gath, rk_v,
    load_sem, sx, rx, sc, rc, sa, ra, sz, rz, sg, rg, sgc, rgc,
):
    f, c = lax.axis_index("feat"), lax.axis_index("rep")
    z, x, y = f // 16, (f // 4) % 4, f % 4

    def in_plane(d):
        i, j = (x + d // 4) % 4, (y + d % 4) % 4
        return 4 * i + j, (z * 16 + 4 * i + j, c)

    def at_z(d):
        return (((z + d) % 8) * 16 + x * 4 + y, c)

    mate = (f, 1 - c)
    barrier = pltpu.get_barrier_semaphore()
    everyone = [mate] + [in_plane(d)[1] for d in range(1, 16)] + [at_z(d) for d in range(1, 8)]
    loads = [
        (in_hbm, x_v.at[0]),
        (phase_hbm, phase_v),
        (freq_hbm, freq_v),
        (w_hbm, w_v),
        (e_hbm, ef_v.at[:, 0:256]),
        (eig_hbm, eig_v),
        (tail_hbm, tail_v),
        (targ_hbm.at[:, 0:384], targ_v.at[0]),
        (targ_hbm.at[:, 384:512], targ_v.at[1, :, 0:128]),
    ]
    loads = [pltpu.make_async_copy(s, d, load_sem.at[i]) for i, (s, d) in enumerate(loads)]
    for load in loads:
        load.start()
    for peer in everyone:
        pl.semaphore_signal(barrier, inc=1, device_id=peer, device_id_type=MESH)

    def remote(src, dst, send, recv, peer):
        return pltpu.make_async_remote_copy(
            src_ref=src, dst_ref=dst, send_sem=send, recv_sem=recv,
            device_id=peer, device_id_type=MESH,
        )

    slot = 4 * x + y

    def core_copy(p):
        return remote(send_c.at[p], recv_c.at[p], sc.at[p], rc.at[p], mate)

    def a_copies(p):
        copies = []
        for d in range(1, 16):
            there, peer = in_plane(d)
            copies.append(remote(buf_a.at[p, there], recv_a.at[p, d - 1], sa.at[p], ra.at[p], peer))
        return copies

    def z_copies(p):
        here = recv_z.at[p, z]
        return [remote(here, here, sz.at[p], rz.at[p], at_z(d)) for d in range(1, 8)]

    def g_copies(p):
        here = gath.at[p, 0, slot]
        return [remote(here, here, sg.at[p], rg.at[p], in_plane(d)[1]) for d in range(1, 16)]

    def a_all(p):
        return remote(recv_a.at[p], recv_a.at[p], sa.at[p], ra.at[p], mate)

    def z_all(p):
        here = recv_z.at[p, 0:7]
        return remote(here, here, sz.at[p], rz.at[p], mate)

    def g_all(p):
        here = gath.at[p, 0, 0:15]
        return remote(here, here, sg.at[p], rg.at[p], mate)

    def gc_copy(p):
        return remote(gath.at[p, 0], gath.at[p, 1], sgc.at[p], rgc.at[p], mate)

    def start(copies):
        for copy in copies:
            copy.start()

    def turn_inputs(half):
        for i in range(4):
            xt_v[half, i * 128:(i + 1) * 128, :] = x_v[half, :, i * 128:(i + 1) * 128].T

    def features(half, rows):
        for n in range(4):
            cols = slice(n * 512, (n + 1) * 512)
            theta = jnp.dot(xt_v[half, rows, :], freq_v[:, cols], preferred_element_type=F32)
            feat_v[half, rows, cols] = scaled_cos(theta, phase_v[:, cols] * INV_TURN)

    def project(half, rows):
        feats = feat_v[half, rows, :]
        on_w = jnp.dot(feats, w_v[...], preferred_element_type=F32)
        return on_w, jnp.dot(feats, ef_v[:, 0:256], preferred_element_type=F32)

    def own_features(n):
        features(0, slice(0, 512))

    def own_project(n):
        rows = slice(n * 256, (n + 1) * 256)
        own_v[rows, 0:512], own_v[rows, 512:768] = project(0, rows)

    def mate_features(p):
        features(1, slice(p * 128, (p + 1) * 128))

    def mate_project(p):
        on_w, on_e = project(1, slice(p * 128, (p + 1) * 128))
        send_c[p, :, 0:512] = on_w.astype(BF)
        send_c[p, :, 512:768] = on_e.astype(BF)
        core_copy(p).start()

    def stage_core(p):
        core_copy(p).wait_recv()
        for i in range(8):
            rows = pl.ds(16 * i, 16)
            here = pl.ds(128 * p + 16 * i, 16)
            total = own_v[here, :] + recv_c[p, rows, :].astype(F32)
            own_v[here, :] = total
            for k in range(2):
                buf_a[p, 2 * i + k] = total[:, 384 * k:384 * (k + 1)].astype(BF)
        start(a_copies(p))
        core_copy(p).wait_send()

    def chunk(ref, first_row):
        rows = pl.ds(pl.multiple_of(first_row + 16 * (slot // 2), 16), 16)
        cols = pl.ds(pl.multiple_of(384 * (slot % 2), 128), 384)
        return ref[rows, cols]

    def stage_plane(p):
        a_all(p).wait_recv()
        total = chunk(own_v, 128 * p)
        for d in range(15):
            total = total + recv_a[p, d].astype(F32)
        recv_z[p, z] = total.astype(BF)
        start(z_copies(p))
        a_all(p).wait_send()

    def stage_line(p):
        z_all(p).wait_recv()
        total = recv_z[p, 0].astype(F32)
        for d in range(1, 8):
            total = total + recv_z[p, d].astype(F32)
        rows = pl.ds(pl.multiple_of(p * 128 + 16 * (slot // 2), 16), 16)
        total = total * scale_v[slot % 2] - targ_v[slot % 2, rows, :].astype(F32)
        gath[p, 0, slot] = total.astype(BF)
        start(g_copies(p))
        z_all(p).wait_send()

    def stage_gather(p):
        g_all(p).wait_recv()
        gc_copy(p).start()
        g_all(p).wait_send()

    column = 4 * f + 2 * c

    def stage_last(p):
        gc_copy(p).wait_recv()
        for half in range(2):
            for b in range(16):
                rows = 256 * p + 128 * half + 16 * (b // 2)
                rk_v[rows:rows + 16, 384 * (b % 2):384 * (b % 2 + 1)] = gath[p, half, b]
        gc_copy(p).wait_send()
        resid = rk_v[256 * p:256 * (p + 1), 0:512]
        pick = lax.broadcasted_iota(jnp.int32, (8, 512), 1) == lax.broadcasted_iota(jnp.int32, (8, 512), 0) + column
        pick = jnp.where(pick, 1.0, 0.0).astype(BF)
        shown = lax.dot_general(pick, resid, (((1,), (1,)), ((), ())), preferred_element_type=F32)
        for half in range(2):
            res_v[half, :, p * 128:(p + 1) * 128] = shown[:, half * 128:(half + 1) * 128]
        coeff = lax.dot_general(
            rk_v[256 * p:256 * (p + 1), 512:768], resid, (((0,), (0,)), ((), ())), preferred_element_type=F32
        )
        if p > 0:
            coeff = coeff + coeff_v[...]
        if p < NP - 1:
            coeff_v[...] = coeff
        else:
            rc_last[0:256, :] = (-coeff).astype(BF)
            rc_last[256:512, :] = resid

    def gradient(n):
        depth = slice(0, 512) if n == 0 else slice(512, 768)
        for i in range(8):
            rows = slice(i * 256, (i + 1) * 256)
            part = jnp.dot(ft_v[rows, depth], rk_v[depth, 0:512], preferred_element_type=F32)
            g_v[rows, :] = part if n == 0 else part + g_v[rows, :]

    def flip(p):
        def tile(n, carry):
            cols = pl.ds(pl.multiple_of(n * 256, 256), 256)
            for half in range(2):
                turned = feat_v[half, p * 128:(p + 1) * 128, cols].T
                if p == NP - 1:
                    ef_v[cols, 256 + half * 128:256 + (half + 1) * 128] = turned
                else:
                    ft_v[cols, p * 256 + half * 128:p * 256 + (half + 1) * 128] = turned
            return carry

        lax.fori_loop(0, 8, tile, 0)

    trade = remote(in_hbm, x_v.at[1], sx, rx, mate)

    def ready(n):
        if n == 0:
            for load in loads[0:3]:
                load.wait()
            turn_inputs(0)
            targ_v[1, :, 128:384] = jnp.zeros((512, 256), BF)
        else:
            for load in loads[3:]:
                load.wait()
            scale_v[...] = jnp.ones_like(scale_v)
            scale_v[1, :, 128:384] = 1.0 - tail_v[0] / eig_v[...]
            rate_v[...] = 1.0 / jnp.full((1, 512), tail_v[0], F32)

    def greet(n):
        pl.semaphore_wait(barrier, len(everyone))
        trade.start()

    def meet(n):
        trade.wait()
        turn_inputs(1)

    steps = dict(
        L=ready, B=greet, T=meet, F=own_features, O=own_project, M=mate_features, P=mate_project,
        X=flip, a=stage_core, b=stage_plane, d=stage_line, f=stage_gather, g=stage_last, G=gradient,
    )
    for op in " ".join(order).split():
        steps[op[0]](int(op[1:]))


def finish(
    w_v, ef_v, g_v, rc_last, shown_v, rate_v,
    out_hbm, res_hbm, out_v, res_v, store_sem,
):
    c = lax.axis_index("rep")
    res_v[:, pl.ds(pl.multiple_of(c * 512, 512), 512)] = shown_v[0, 0:2, :]
    res_v[:, pl.ds(pl.multiple_of((1 - c) * 512, 512), 512)] = shown_v[1, 0:2, :]
    show = pltpu.make_async_copy(res_v, res_hbm, store_sem.at[8])
    show.start()

    copies = [show]
    for n in range(8):
        rows = slice(n * 256, (n + 1) * 256)
        part = jnp.dot(ef_v[rows, :], rc_last[...], preferred_element_type=F32) + g_v[rows, :]
        out_v[rows, :] = (w_v[rows, :].astype(F32) - part * rate_v[...]).astype(BF)
        copies.append(pltpu.make_async_copy(out_v.at[rows], out_hbm.at[rows], store_sem.at[n]))
        copies[-1].start()
    for copy in copies:
        copy.wait()


ORDER = (
    "L0 F0 B0 L1", "O0 T0 M0 P0", "O1 a0 M1 P1", "M2 P2 a1", "M3 P3 a2", "X0 a3 X1", "b0 X2 b1 X3", "b2 b3",
    "d0 d1 d2 d3", "f0 f1 g0", "f2 g1 G0", "f3 g2 G1 g3",
)


def shards(inputs, targets, frequencies, phases, weights, eigvecs, eigvals, tail):
    hbm = pl.BlockSpec(memory_space=pl.ANY)
    vmem = pl.BlockSpec(memory_space=pltpu.VMEM)
    dma = pltpu.SemaphoreType.DMA
    chunk = (16, 384)
    kept = pl.pallas_call(
        functools.partial(kernel, ORDER),
        out_shape=[
            pltpu.VMEM((2048, 512), BF),
            pltpu.VMEM((2048, 512), BF),
            pltpu.VMEM((2048, 512), F32),
            pltpu.VMEM((512, 512), BF),
            pltpu.VMEM((2, 8, 512), F32),
            pltpu.VMEM((1, 512), F32),
        ],
        in_specs=[hbm] * 8,
        out_specs=[vmem] * 6,
        scratch_shapes=[
            pltpu.VMEM((2, 440, 512), BF),
            pltpu.VMEM((440, 2048), BF),
            pltpu.VMEM((2, 512, 384), BF),
            pltpu.VMEM((2, 1, 384), F32),
            pltpu.VMEM((2, 512, 2048), BF),
            pltpu.VMEM((2048, 768), BF),
            pltpu.VMEM((256, 512), F32),
            pltpu.VMEM((1, 2048), F32),
            pltpu.VMEM((1, 256), F32),
            pltpu.SMEM((1,), F32),
            pltpu.VMEM((2, 512, 440), BF),
            pltpu.VMEM((512, 768), F32),
            pltpu.VMEM((NP, 128, 768), BF),
            pltpu.VMEM((NP, 128, 768), BF),
            pltpu.VMEM((NP, 16) + chunk, BF),
            pltpu.VMEM((NP, 15) + chunk, BF),
            pltpu.VMEM((NP, 8) + chunk, BF),
            pltpu.VMEM((NP, 2, 16) + chunk, BF),
            pltpu.VMEM((1024, 768), BF),
            dma((9,)),
            dma, dma,
            dma((NP,)), dma((NP,)),
            dma((NP,)), dma((NP,)),
            dma((NP,)), dma((NP,)),
            dma((NP,)), dma((NP,)),
            dma((NP,)), dma((NP,)),
        ],
        compiler_params=pltpu.CompilerParams(
            collective_id=0, has_side_effects=True, vmem_limit_bytes=48 << 20
        ),
        name="step",
    )(
        inputs.T, targets, frequencies, weights, eigvecs,
        phases.reshape(1, -1), eigvals.reshape(1, -1), tail,
    )
    new_weights, residual = pl.pallas_call(
        finish,
        out_shape=[jax.ShapeDtypeStruct((2048, 512), BF), jax.ShapeDtypeStruct((2, 1024), F32)],
        in_specs=[vmem] * 6,
        out_specs=[hbm, hbm],
        scratch_shapes=[pltpu.VMEM((2048, 512), BF), pltpu.VMEM((2, 1024), F32), dma((9,))],
        compiler_params=pltpu.CompilerParams(vmem_limit_bytes=16 << 20),
        name="finish",
    )(*kept)
    return (new_weights, residual.T)


def solution(mesh):
    in_specs = (
        P("rep", None),
        P("rep", None),
        P(None, ("feat", "rep")),
        P(("feat", "rep")),
        P(("feat", "rep"), None),
        P(("feat", "rep"), None),
        P(),
        P(),
    )
    out_specs = (P(("feat", "rep"), None), P(None, ("feat", "rep")))
    return jax.shard_map(shards, mesh=mesh, in_specs=in_specs, out_specs=out_specs, check_vma=False)
```

```python
import functools
import math

import jax
import jax.numpy as jnp
from jax import lax
from jax.experimental import pallas as pl
from jax.experimental.pallas import tpu as pltpu
from jax.sharding import PartitionSpec as P

MESH = pl.DeviceIdType.MESH
BF, F32 = jnp.bfloat16, jnp.float32
FEATURES = 524288
SCALE = math.sqrt(2.0 / FEATURES)
INV_TURN = 1.0 / (2.0 * math.pi)
SIN = (6.283164044300404, -41.33714237083565, 81.34076887918835, -70.99343319450264)
NP = 4


def scaled_cos(theta, turns):
    t = theta * INV_TURN + turns
    s = 0.25 - jnp.abs(t - jnp.round(t))
    u = s * s
    p = SIN[3] * SCALE
    for q in SIN[2::-1]:
        p = p * u + q * SCALE
    return (s * p).astype(BF)


def kernel(
    order, in_hbm, targ_hbm, freq_hbm, w_hbm, e_hbm, phase_hbm, eig_hbm, tail_hbm,
    w_v, ef_v, g_v, rc_last, res_v, rate_v,
    x_v, freq_v, targ_v, scale_v, feat_v, ft_v, coeff_v, phase_v, eig_v, tail_v,
    xt_v, own_v, send_c, recv_c, buf_a, recv_a, recv_z, gath, rk_v,
    load_sem, sx, rx, sc, rc, sa, ra, sz, rz, sg, rg, sgc, rgc,
):
    f, c = lax.axis_index("feat"), lax.axis_index("rep")
    z, x, y = f // 16, (f // 4) % 4, f % 4

    def in_plane(d):
        i, j = (x + d // 4) % 4, (y + d % 4) % 4
        return 4 * i + j, (z * 16 + 4 * i + j, c)

    def at_z(d):
        return (((z + d) % 8) * 16 + x * 4 + y, c)

    mate = (f, 1 - c)
    barrier = pltpu.get_barrier_semaphore()
    everyone = [mate] + [in_plane(d)[1] for d in range(1, 16)] + [at_z(d) for d in range(1, 8)]
    loads = [
        (in_hbm, x_v.at[0]),
        (phase_hbm, phase_v),
        (freq_hbm, freq_v),
        (w_hbm, w_v),
        (e_hbm, ef_v.at[:, 0:256]),
        (eig_hbm, eig_v),
        (tail_hbm, tail_v),
        (targ_hbm.at[:, 0:384], targ_v.at[0]),
        (targ_hbm.at[:, 384:512], targ_v.at[1, :, 0:128]),
    ]
    loads = [pltpu.make_async_copy(s, d, load_sem.at[i]) for i, (s, d) in enumerate(loads)]
    for load in loads:
        load.start()
    for peer in everyone:
        pl.semaphore_signal(barrier, inc=1, device_id=peer, device_id_type=MESH)

    def remote(src, dst, send, recv, peer):
        return pltpu.make_async_remote_copy(
            src_ref=src, dst_ref=dst, send_sem=send, recv_sem=recv,
            device_id=peer, device_id_type=MESH,
        )

    slot = 4 * x + y

    def core_copy(p):
        return remote(send_c.at[p], recv_c.at[p], sc.at[p], rc.at[p], mate)

    def a_copies(p):
        copies = []
        for d in range(1, 16):
            there, peer = in_plane(d)
            copies.append(remote(buf_a.at[p, there], recv_a.at[p, d - 1], sa.at[p], ra.at[p], peer))
        return copies

    def z_copies(p):
        here = recv_z.at[p, z]
        return [remote(here, here, sz.at[p], rz.at[p], at_z(d)) for d in range(1, 8)]

    def g_copies(p):
        here = gath.at[p, 0, slot]
        return [remote(here, here, sg.at[p], rg.at[p], in_plane(d)[1]) for d in range(1, 16)]

    def a_all(p):
        return remote(recv_a.at[p], recv_a.at[p], sa.at[p], ra.at[p], mate)

    def z_all(p):
        here = recv_z.at[p, 0:7]
        return remote(here, here, sz.at[p], rz.at[p], mate)

    def g_all(p):
        here = gath.at[p, 0, 0:15]
        return remote(here, here, sg.at[p], rg.at[p], mate)

    def gc_copy(p):
        return remote(gath.at[p, 0], gath.at[p, 1], sgc.at[p], rgc.at[p], mate)

    def start(copies):
        for copy in copies:
            copy.start()

    def turn_inputs(half):
        for i in range(4):
            xt_v[half, i * 128:(i + 1) * 128, :] = x_v[half, :, i * 128:(i + 1) * 128].T

    def features(half, rows):
        for n in range(4):
            cols = slice(n * 512, (n + 1) * 512)
            theta = jnp.dot(xt_v[half, rows, :], freq_v[:, cols], preferred_element_type=F32)
            feat_v[half, rows, cols] = scaled_cos(theta, phase_v[:, cols] * INV_TURN)

    def project(half, rows):
        feats = feat_v[half, rows, :]
        on_w = jnp.dot(feats, w_v[...], preferred_element_type=F32)
        return on_w, jnp.dot(feats, ef_v[:, 0:256], preferred_element_type=F32)

    def own_features(n):
        features(0, slice(0, 512))

    def own_project(n):
        rows = slice(n * 128, (n + 1) * 128)
        own_v[rows, 0:512], own_v[rows, 512:768] = project(0, rows)

    def mate_features(p):
        features(1, slice(p * 128, (p + 1) * 128))

    def mate_project(p):
        on_w, on_e = project(1, slice(p * 128, (p + 1) * 128))
        send_c[p, :, 0:512] = on_w.astype(BF)
        send_c[p, :, 512:768] = on_e.astype(BF)
        core_copy(p).start()

    def stage_core(p):
        core_copy(p).wait_recv()
        for i in range(8):
            rows = pl.ds(16 * i, 16)
            here = pl.ds(128 * p + 16 * i, 16)
            total = own_v[here, :] + recv_c[p, rows, :].astype(F32)
            own_v[here, :] = total
            for k in range(2):
                buf_a[p, 2 * i + k] = total[:, 384 * k:384 * (k + 1)].astype(BF)
        start(a_copies(p))
        core_copy(p).wait_send()

    def chunk(ref, first_row):
        rows = pl.ds(pl.multiple_of(first_row + 16 * (slot // 2), 16), 16)
        cols = pl.ds(pl.multiple_of(384 * (slot % 2), 128), 384)
        return ref[rows, cols]

    def stage_plane(p):
        a_all(p).wait_recv()
        total = chunk(own_v, 128 * p)
        for d in range(15):
            total = total + recv_a[p, d].astype(F32)
        recv_z[p, z] = total.astype(BF)
        start(z_copies(p))
        a_all(p).wait_send()

    def stage_line(p):
        z_all(p).wait_recv()
        total = recv_z[p, 0].astype(F32)
        for d in range(1, 8):
            total = total + recv_z[p, d].astype(F32)
        rows = pl.ds(pl.multiple_of(p * 128 + 16 * (slot // 2), 16), 16)
        total = total * scale_v[slot % 2] - targ_v[slot % 2, rows, :].astype(F32)
        gath[p, 0, slot] = total.astype(BF)
        start(g_copies(p))
        z_all(p).wait_send()

    def stage_gather(p):
        g_all(p).wait_recv()
        gc_copy(p).start()
        g_all(p).wait_send()

    column = 4 * f + 2 * c

    def stage_last(p):
        gc_copy(p).wait_recv()
        for half in range(2):
            for b in range(16):
                rows = 256 * p + 128 * half + 16 * (b // 2)
                rk_v[rows:rows + 16, 384 * (b % 2):384 * (b % 2 + 1)] = gath[p, half, b]
        gc_copy(p).wait_send()
        resid = rk_v[256 * p:256 * (p + 1), 0:512]
        pick = lax.broadcasted_iota(jnp.int32, (8, 512), 1) == lax.broadcasted_iota(jnp.int32, (8, 512), 0) + column
        pick = jnp.where(pick, 1.0, 0.0).astype(BF)
        shown = lax.dot_general(pick, resid, (((1,), (1,)), ((), ())), preferred_element_type=F32)
        for half in range(2):
            res_v[half, :, p * 128:(p + 1) * 128] = shown[:, half * 128:(half + 1) * 128]
        coeff = lax.dot_general(
            rk_v[256 * p:256 * (p + 1), 512:768], resid, (((0,), (0,)), ((), ())), preferred_element_type=F32
        )
        if p > 0:
            coeff = coeff + coeff_v[...]
        if p < NP - 1:
            coeff_v[...] = coeff
        else:
            rc_last[0:256, :] = (-coeff).astype(BF)
            rc_last[256:512, :] = resid

    def gradient(n):
        depth = slice(0, 512) if n == 0 else slice(512, 768)
        for i in range(8):
            rows = slice(i * 256, (i + 1) * 256)
            part = jnp.dot(ft_v[rows, depth], rk_v[depth, 0:512], preferred_element_type=F32)
            g_v[rows, :] = part if n == 0 else part + g_v[rows, :]

    def flip(p):
        def tile(n, carry):
            cols = pl.ds(pl.multiple_of(n * 256, 256), 256)
            for half in range(2):
                turned = feat_v[half, p * 128:(p + 1) * 128, cols].T
                if p == NP - 1:
                    ef_v[cols, 256 + half * 128:256 + (half + 1) * 128] = turned
                else:
                    ft_v[cols, p * 256 + half * 128:p * 256 + (half + 1) * 128] = turned
            return carry

        lax.fori_loop(0, 8, tile, 0)

    trade = remote(in_hbm, x_v.at[1], sx, rx, mate)

    def ready(n):
        if n == 0:
            for load in loads[0:3]:
                load.wait()
            turn_inputs(0)
            targ_v[1, :, 128:384] = jnp.zeros((512, 256), BF)
        else:
            for load in loads[3:]:
                load.wait()
            scale_v[...] = jnp.ones_like(scale_v)
            scale_v[1, :, 128:384] = 1.0 - tail_v[0] / eig_v[...]
            rate_v[...] = 1.0 / jnp.full((1, 512), tail_v[0], F32)

    def greet(n):
        pl.semaphore_wait(barrier, len(everyone))
        trade.start()

    def meet(n):
        trade.wait()
        turn_inputs(1)

    steps = dict(
        L=ready, B=greet, T=meet, F=own_features, O=own_project, M=mate_features, P=mate_project,
        X=flip, a=stage_core, b=stage_plane, d=stage_line, f=stage_gather, g=stage_last, G=gradient,
    )
    for op in " ".join(order).split():
        steps[op[0]](int(op[1:]))


def finish(
    w_v, ef_v, g_v, rc_last, shown_v, rate_v,
    out_hbm, res_hbm, out_v, res_v, store_sem,
):
    c = lax.axis_index("rep")
    res_v[:, pl.ds(pl.multiple_of(c * 512, 512), 512)] = shown_v[0, 0:2, :]
    res_v[:, pl.ds(pl.multiple_of((1 - c) * 512, 512), 512)] = shown_v[1, 0:2, :]
    show = pltpu.make_async_copy(res_v, res_hbm, store_sem.at[8])
    show.start()

    copies = [show]
    for n in range(8):
        rows = slice(n * 256, (n + 1) * 256)
        part = jnp.dot(ef_v[rows, :], rc_last[...], preferred_element_type=F32) + g_v[rows, :]
        out_v[rows, :] = (w_v[rows, :].astype(F32) - part * rate_v[...]).astype(BF)
        copies.append(pltpu.make_async_copy(out_v.at[rows], out_hbm.at[rows], store_sem.at[n]))
        copies[-1].start()
    for copy in copies:
        copy.wait()


ORDER = (
    "L0 F0 B0 L1", "O0 O1 T0 M0", "P0 M1 P1 a0", "M2 P2 a1 O2", "M3 P3 a2 O3", "a3 X0 X1 b0", "X2 b1 X3 b2", "b3",
    "d0 d1 d2 d3", "f0 f1 g0", "f2 g1 G0", "f3 g2 G1 g3",
)


def shards(inputs, targets, frequencies, phases, weights, eigvecs, eigvals, tail):
    hbm = pl.BlockSpec(memory_space=pl.ANY)
    vmem = pl.BlockSpec(memory_space=pltpu.VMEM)
    dma = pltpu.SemaphoreType.DMA
    chunk = (16, 384)
    kept = pl.pallas_call(
        functools.partial(kernel, ORDER),
        out_shape=[
            pltpu.VMEM((2048, 512), BF),
            pltpu.VMEM((2048, 512), BF),
            pltpu.VMEM((2048, 512), F32),
            pltpu.VMEM((512, 512), BF),
            pltpu.VMEM((2, 8, 512), F32),
            pltpu.VMEM((1, 512), F32),
        ],
        in_specs=[hbm] * 8,
        out_specs=[vmem] * 6,
        scratch_shapes=[
            pltpu.VMEM((2, 440, 512), BF),
            pltpu.VMEM((440, 2048), BF),
            pltpu.VMEM((2, 512, 384), BF),
            pltpu.VMEM((2, 1, 384), F32),
            pltpu.VMEM((2, 512, 2048), BF),
            pltpu.VMEM((2048, 768), BF),
            pltpu.VMEM((256, 512), F32),
            pltpu.VMEM((1, 2048), F32),
            pltpu.VMEM((1, 256), F32),
            pltpu.SMEM((1,), F32),
            pltpu.VMEM((2, 512, 440), BF),
            pltpu.VMEM((512, 768), F32),
            pltpu.VMEM((NP, 128, 768), BF),
            pltpu.VMEM((NP, 128, 768), BF),
            pltpu.VMEM((NP, 16) + chunk, BF),
            pltpu.VMEM((NP, 15) + chunk, BF),
            pltpu.VMEM((NP, 8) + chunk, BF),
            pltpu.VMEM((NP, 2, 16) + chunk, BF),
            pltpu.VMEM((1024, 768), BF),
            dma((9,)),
            dma, dma,
            dma((NP,)), dma((NP,)),
            dma((NP,)), dma((NP,)),
            dma((NP,)), dma((NP,)),
            dma((NP,)), dma((NP,)),
            dma((NP,)), dma((NP,)),
        ],
        compiler_params=pltpu.CompilerParams(
            collective_id=0, has_side_effects=True, vmem_limit_bytes=48 << 20
        ),
        name="step",
    )(
        inputs.T, targets, frequencies, weights, eigvecs,
        phases.reshape(1, -1), eigvals.reshape(1, -1), tail,
    )
    new_weights, residual = pl.pallas_call(
        finish,
        out_shape=[jax.ShapeDtypeStruct((2048, 512), BF), jax.ShapeDtypeStruct((2, 1024), F32)],
        in_specs=[vmem] * 6,
        out_specs=[hbm, hbm],
        scratch_shapes=[pltpu.VMEM((2048, 512), BF), pltpu.VMEM((2, 1024), F32), dma((9,))],
        compiler_params=pltpu.CompilerParams(vmem_limit_bytes=16 << 20),
        name="finish",
    )(*kept)
    return (new_weights, residual.T)


def solution(mesh):
    in_specs = (
        P("rep", None),
        P("rep", None),
        P(None, ("feat", "rep")),
        P(("feat", "rep")),
        P(("feat", "rep"), None),
        P(("feat", "rep"), None),
        P(),
        P(),
    )
    out_specs = (P(("feat", "rep"), None), P(None, ("feat", "rep")))
    return jax.shard_map(shards, mesh=mesh, in_specs=in_specs, out_specs=out_specs, check_vma=False)
```
